32 devices in a mesh: ka: 8 (over z, core), row: 4 (over y, x).
Axes of the slice: x: 2, y: 2, z: 4, core: 2. Of those that a mesh axis runs over, the one named last changes fastest.
Arguments:
- frames: bfloat16 [2, 1024, 64, 256], P(None, 'ka', 'row'), may hold values from -16 to 16
Outputs:
- decorrelation: float32 [512, 64, 256], P('ka', 'row')
The draws below stay inside these ranges and needn't reach their ends.
All inputs are finite; a program needn't handle non-finite values.
Results may differ from the reference program's by a relative error of at most 0.002.
Values may be sent and summed in bfloat16 or wider, within the bound.
No kernel may reach another device: no remote copies, remote signals or barrier semaphores. Data moves between devices by JAX's collectives and lax.ppermute only.
A program may use at most 128 MiB of HBM per device.

```python
import math
import jax
import jax.numpy as jnp
from jax import lax

K = 1024
COLS = 256
DEPTH = 512
ROWS = 64


def draw_frames(key, part):
    key = jax.random.fold_in(key, 7)
    first_key, second_key, mix_key = jax.random.split(key, 3)
    base = jax.random.normal(first_key, (K, ROWS, COLS), jnp.float32)
    noise = jax.random.normal(second_key, (K, ROWS, COLS), jnp.float32)
    mixing = jax.random.uniform(mix_key, (1, ROWS, COLS), jnp.float32, 0.0, 1.0)
    second = mixing * base + jnp.sqrt(1.0 - mixing * mixing) * noise
    both = jnp.stack((base, second), axis=0)
    return jnp.clip(both, -16.0, 16.0).astype(jnp.bfloat16)


def setup_inputs(seed: int = 0) -> dict:
    key_of = jax.random.split(jax.random.key(seed), 2)
    return {
        "frames": draw_frames(jax.random.fold_in(key_of[1], 71), 0),
    }


def dft_tables(size, depths):
    kpos = jnp.arange(size, dtype=jnp.int32)
    zpos = jnp.arange(depths, dtype=jnp.int32)
    phase = kpos[:, None] * zpos[None, :] % size
    angle = phase.astype(jnp.float32) * (2.0 * math.pi / size)
    return (jnp.cos(angle).astype(jnp.bfloat16), jnp.sin(angle).astype(jnp.bfloat16))

def reference(frames):
    cos_table, sin_table = dft_tables(K, DEPTH)
    cos_wide = cos_table.astype(jnp.float32)
    sin_wide = sin_table.astype(jnp.float32)
    scale = float(K) ** (-0.5)
    by_row = jnp.moveaxis(frames, 2, 0)

    def one_row(samples):
        wide = samples.astype(jnp.float32)
        real = jnp.einsum('kz,pkc->zpc', cos_wide, wide, precision=lax.Precision.HIGHEST)
        imag = -jnp.einsum('kz,pkc->zpc', sin_wide, wide, precision=lax.Precision.HIGHEST)
        both = jnp.stack((real, imag), axis=2) * scale
        return both.reshape(both.shape[0], 4, both.shape[3]).astype(jnp.bfloat16)
    spectra = lax.map(one_row, by_row)
    spectrum = jnp.transpose(spectra, (1, 2, 0, 3)).astype(jnp.float32)
    a_one, b_one = (spectrum[:, 0], spectrum[:, 1])
    a_two, b_two = (spectrum[:, 2], spectrum[:, 3])
    cross_re = a_one * a_two + b_one * b_two
    cross_im = b_one * a_two - a_one * b_two
    power = (a_one * a_one + b_one * b_one + a_two * a_two + b_two * b_two) / 2.0
    terms = jnp.stack((cross_re, cross_im, power), axis=0)
    padded = jnp.pad(terms, ((0, 0), (1, 1), (1, 1), (1, 1)))
    summed = padded[:, :-2] + padded[:, 1:-1] + padded[:, 2:]
    summed = summed[:, :, :-2] + summed[:, :, 1:-1] + summed[:, :, 2:]
    summed = summed[:, :, :, :-2] + summed[:, :, :, 1:-1] + summed[:, :, :, 2:]
    magnitude = jnp.sqrt(summed[0] * summed[0] + summed[1] * summed[1])
    return 1.0 - magnitude / (summed[2] + 1e-05)
```

```python
import functools
import math

import jax
import jax.numpy as jnp
import numpy as np
from jax import lax
from jax.experimental import pallas as pl
from jax.experimental.pallas import tpu as pltpu
from jax.sharding import PartitionSpec as P

K = 1024
DEPTH = 512
LANES = 128
EDGE = 16
F32 = jnp.float32
BF16 = jnp.bfloat16


def table():
    phase = (np.arange(K)[None, :] * np.arange(DEPTH)[:, None]) % K
    angle = phase.astype(np.float32) * np.float32(2.0 * math.pi / K)
    both = np.concatenate([np.cos(angle), np.sin(angle)], axis=0)
    return both.astype(jnp.bfloat16)


def place(dest, half, rb, mirrored):
    h = dest // half
    q = dest % half
    q = jnp.where(mirrored, half - 1 - q, q)
    return h, q * rb


def params(mib=48):
    return pltpu.CompilerParams(vmem_limit_bytes=mib * 1024 * 1024)


def split_kernel(n, rows, kl, rb, first, rest, x_ref, *refs):
    half = n // 2
    a_refs, b_refs = refs[:n], refs[n : n + (n if rest else 0)]
    x32, e_scr, e16 = refs[-3:]
    me = lax.axis_index("ka")
    mirrored = lax.axis_index("row") % 2 == 1
    x32[0] = x_ref[:, :LANES].astype(F32)
    x32[1] = x_ref[:, LANES:].astype(F32)
    lane = lax.broadcasted_iota(jnp.int32, (kl, LANES), 1)
    for h in range(2):
        m = jnp.zeros((kl, LANES), F32)
        for p in range(2):
            for r in range(rows):
                at = p * rows + r
                y = x32[1 - h, pl.ds(p * kl * rows + r, kl, stride=rows), :]
                m = jnp.where(lane == at, pltpu.roll(y, (at + h) % LANES, 1), m)
        if kl < LANES:
            m = jnp.concatenate([m, jnp.zeros((LANES - kl, LANES), F32)], axis=0)
        e_scr[h] = m.T
    e16[...] = jnp.zeros_like(e16)
    for s in range(n):
        h, row = place(me ^ s, half, rb, mirrored)
        for out, group in ((a_refs, first), (b_refs, rest)):
            for slot, j in enumerate(group):
                for p in range(2):
                    y = x32[h, pl.ds(p * kl * rows + row + j, kl, stride=rows), :]
                    out[s][pl.ds((slot * 2 + p) * kl, kl), :] = y.astype(BF16)
        for p in range(2):
            e16[pl.ds(p * 8 + 1, rb), :] = e_scr[h, pl.ds(p * rows + row, rb), :]
        a_refs[s][pl.ds(len(first) * 2 * kl, EDGE), :] = e16[...].astype(BF16)


def split(x, n, rows, kl, rb, first, rest):
    a_shape = jax.ShapeDtypeStruct((len(first) * 2 * kl + EDGE, LANES), BF16)
    b_shape = jax.ShapeDtypeStruct((len(rest) * 2 * kl, LANES), BF16)
    out = pl.pallas_call(
        functools.partial(split_kernel, n, rows, kl, rb, first, rest),
        out_shape=[a_shape] * n + ([b_shape] * n if rest else []),
        scratch_shapes=[
            pltpu.VMEM((2, 2 * kl * rows, LANES), F32),
            pltpu.VMEM((2, LANES, LANES), F32),
            pltpu.VMEM((EDGE, LANES), F32),
        ],
        compiler_params=params(),
        cost_estimate=pl.CostEstimate(flops=10**6, bytes_accessed=4 * 2**20, transcendentals=0),
        name="split",
    )(x)
    return out[:n], out[n:]


def gather(n, refs, held, sem):
    me = lax.axis_index("ka")
    copies = [
        pltpu.make_async_copy(refs[s], held.at[me ^ s], sem.at[s]) for s in range(n)
    ]
    for c in copies:
        c.start()
    for c in copies:
        c.wait()


def samples(held, n, kl, slot):
    return jnp.concatenate(
        [
            held[:, (slot * 2 + p) * kl : (slot * 2 + p + 1) * kl, :].reshape(n * kl, LANES)
            for p in range(2)
        ],
        axis=1,
    )


def rounded(x):
    return (x * (float(K) ** -0.5)).astype(BF16)


def outer_kernel(n, kl, first, *refs):
    pieces, t_ref = refs[:n], refs[n]
    outs = refs[n + 1 : n + 1 + len(first)]
    held, sem = refs[-2:]
    gather(n, pieces, held, sem)
    base = len(first) * 2 * kl
    e = jnp.concatenate([held[j, base : base + EDGE, :kl] for j in range(n)], axis=1)
    e = jnp.concatenate([e, jnp.zeros((LANES - EDGE, K), BF16)], axis=0)
    se = lax.dot_general(t_ref[...], e, (((1,), (1,)), ((), ())), preferred_element_type=F32)
    se = rounded(se).astype(F32)
    packed = se[:LANES]
    for b in range(1, 2 * DEPTH // LANES):
        packed = packed + pltpu.roll(se[b * LANES : (b + 1) * LANES], EDGE * b, 1)
    packed = packed.astype(BF16)
    for slot in range(len(first)):
        s = rounded(jnp.dot(t_ref[...], samples(held, n, kl, slot), preferred_element_type=F32))
        outs[slot][: 2 * DEPTH, :] = s[:, :LANES]
        outs[slot][2 * DEPTH : 4 * DEPTH, :] = s[:, LANES:]
        outs[slot][4 * DEPTH :, :] = packed


def outer(pieces, t, n, kl, first):
    return pl.pallas_call(
        functools.partial(outer_kernel, n, kl, first),
        out_shape=[jax.ShapeDtypeStruct((4 * DEPTH + LANES, LANES), BF16)] * len(first),
        in_specs=[pl.BlockSpec(memory_space=pl.ANY)] * n + [pl.BlockSpec(memory_space=pltpu.VMEM)],
        scratch_shapes=[
            pltpu.VMEM((n, len(first) * 2 * kl + EDGE, LANES), BF16),
            pltpu.SemaphoreType.DMA((n,)),
        ],
        compiler_params=params(),
        cost_estimate=pl.CostEstimate(
            flops=2 * 2 * DEPTH * K * 256 * 3, bytes_accessed=4 * 2**20, transcendentals=0
        ),
        name="outer",
    )(*pieces, t)


def terms(a1, b1, a2, b2):
    re = a1 * a2 + b1 * b2
    im = b1 * a2 - a1 * b2
    pw = (a1 * a1 + b1 * b1 + a2 * a2 + b2 * b2) * 0.5
    return re, im, pw


def inner_kernel(n, kl, rb, rest, *refs):
    nb = n if rest else 0
    pieces = refs[:nb]
    t_ref, top, bottom, above, below = refs[nb : nb + 5]
    outs = refs[nb + 5 : nb + 5 + n]
    held, sem, prod, edge, zpad, dec = refs[-6:]
    half = n // 2
    me = lax.axis_index("ka")
    h = me // half
    dl = DEPTH // n
    if rest:
        gather(n, pieces, held, sem)

    for at, ref in ((0, above), (1, top), (rb, bottom), (rb + 1, below)):
        @pl.loop(0, DEPTH // 64)
        def _(i):
            z = pl.multiple_of(i * 64, 64)
            parts = [
                ref[pl.ds(z + off, 64), :].astype(F32)
                for off in (0, DEPTH, 2 * DEPTH, 3 * DEPTH)
            ]
            for t, v in enumerate(terms(*parts)):
                prod[at, t, pl.ds(z, 64), :] = v
    for slot, r in enumerate(rest):
        s = rounded(
            jnp.dot(t_ref[...], samples(held, n, kl, slot), preferred_element_type=F32)
        ).astype(F32)
        a, b = s[:DEPTH], s[DEPTH:]
        for t, v in enumerate(terms(a[:, :LANES], b[:, :LANES], a[:, LANES:], b[:, LANES:])):
            prod[r + 1, t] = v

    lane = lax.broadcasted_iota(jnp.int32, (LANES, LANES), 1)
    mine = top[4 * DEPTH :, :].astype(F32)
    up = pltpu.roll(above[4 * DEPTH :, :].astype(F32), LANES - rb, 1)
    down = pltpu.roll(below[4 * DEPTH :, :].astype(F32), rb, 1)
    mine = jnp.where(lane % 8 == 0, up, jnp.where(lane % 8 == rb + 1, down, mine))
    blocks = DEPTH // LANES
    for b in range(blocks):
        c = mine if b == 0 else pltpu.roll(mine, LANES - EDGE * b, 1)
        s = pltpu.roll(mine, LANES - EDGE * (b + blocks), 1)
        c2, s2 = pltpu.roll(c, LANES - 8, 1), pltpu.roll(s, LANES - 8, 1)
        for t, v in enumerate(terms(c, s, c2, s2)):
            v = v + pltpu.roll(v, 1, 1) + pltpu.roll(v, LANES - 1, 1)
            edge[t, pl.ds(b * LANES, LANES), :] = v

    zero8 = jnp.zeros((8, LANES), F32)
    for t in range(3):
        zpad[t, pl.ds(0, 8), :] = zero8
        zpad[t, pl.ds(DEPTH + 8, 8), :] = zero8
    lane = lax.broadcasted_iota(jnp.int32, (64, LANES), 1)
    not_first, not_last = lane > 0, lane < LANES - 1
    at_edge = lane == jnp.where(h == 0, LANES - 1, 0)
    for r in range(rb):
        shift = LANES - 2 - r + h

        @pl.loop(0, DEPTH // 64)
        def _(i):
            z = pl.multiple_of(i * 64, 64)
            for t in range(3):
                v = (
                    prod[r, t, pl.ds(z, 64), :]
                    + prod[r + 1, t, pl.ds(z, 64), :]
                    + prod[r + 2, t, pl.ds(z, 64), :]
                )
                left = jnp.where(not_first, pltpu.roll(v, 1, 1), 0.0)
                right = jnp.where(not_last, pltpu.roll(v, LANES - 1, 1), 0.0)
                e = jnp.where(at_edge, pltpu.roll(edge[t, pl.ds(z, 64), :], shift, 1), 0.0)
                zpad[t, pl.ds(z + 8, 64), :] = v + left + right + e

        @pl.loop(0, DEPTH // 64)
        def _(i):
            z = pl.multiple_of(i * 64, 64)
            box = [
                zpad[t, pl.ds(z + 7, 64), :]
                + zpad[t, pl.ds(z + 8, 64), :]
                + zpad[t, pl.ds(z + 9, 64), :]
                for t in range(3)
            ]
            magnitude = jnp.sqrt(box[0] * box[0] + box[1] * box[1])
            dec[r, pl.ds(z, 64), :] = 1.0 - magnitude / (box[2] + 1e-05)

    for s in range(n):
        z = pl.multiple_of((me ^ s) * dl, dl)
        for r in range(rb):
            outs[s][pl.ds(r * dl, dl), :] = dec[r, pl.ds(z, dl), :].astype(BF16)


def inner(pieces, t, halos, n, kl, rb, rest):
    nb = n if rest else 0
    return pl.pallas_call(
        functools.partial(inner_kernel, n, kl, rb, rest),
        out_shape=[jax.ShapeDtypeStruct((rb * (DEPTH // n), LANES), BF16)] * n,
        in_specs=[pl.BlockSpec(memory_space=pl.ANY)] * nb
        + [pl.BlockSpec(memory_space=pltpu.VMEM)] * 5,
        scratch_shapes=[
            pltpu.VMEM((n, max(len(rest) * 2 * kl, 16), LANES), BF16),
            pltpu.SemaphoreType.DMA((n,)),
            pltpu.VMEM((rb + 2, 3, DEPTH, LANES), F32),
            pltpu.VMEM((3, DEPTH, LANES), F32),
            pltpu.VMEM((3, DEPTH + 16, LANES), F32),
            pltpu.VMEM((rb, DEPTH, LANES), F32),
        ],
        compiler_params=params(),
        cost_estimate=pl.CostEstimate(
            flops=2 * 2 * DEPTH * K * 256 * len(rest) + 10**7,
            bytes_accessed=6 * 2**20,
            transcendentals=0,
        ),
        name="inner",
    )(*pieces, t, *halos)


def join_kernel(n, rows, rb, *refs):
    half = n // 2
    pieces, out, held = refs[:n], refs[n], refs[n + 1]
    me = lax.axis_index("ka")
    mirrored = lax.axis_index("row") % 2 == 1
    dl = DEPTH // n
    for s in range(n):
        h, row = place(me ^ s, half, rb, mirrored)
        for r in range(rb):
            d = pieces[s][pl.ds(r * dl, dl), :].astype(F32)
            held[h, pl.ds(row + r, dl, stride=rows), :] = d
    out[:, :LANES] = held[0]
    out[:, LANES:] = held[1]


def join(pieces, n, rows, rb):
    return pl.pallas_call(
        functools.partial(join_kernel, n, rows, rb),
        out_shape=jax.ShapeDtypeStruct((DEPTH // n * rows, 2 * LANES), F32),
        scratch_shapes=[pltpu.VMEM((2, DEPTH // n * rows, LANES), F32)],
        compiler_params=params(),
        cost_estimate=pl.CostEstimate(flops=10**6, bytes_accessed=2 * 2**20, transcendentals=0),
        name="join",
    )(*pieces)


def body(frames):
    n, groups = lax.axis_size("ka"), lax.axis_size("row")
    _, kl, rows, cols = frames.shape
    half = n // 2
    rb = rows // half
    first, rest = (0, rb - 1), tuple(range(1, rb - 1))
    t = jnp.asarray(table())

    order = sorted(range(1, n), key=lambda s: (s & half) == 0)

    def exchange(pieces):
        out = list(pieces)
        for s in order:
            out[s] = lax.ppermute(pieces[s], "ka", [(i, i ^ s) for i in range(n)])
        return out

    a, b = split(frames.reshape(2 * kl * rows, cols), n, rows, kl, rb, first, rest)
    a = exchange(a)
    b = exchange(b) if rest else []
    top, bottom = outer(a, t, n, kl, first)

    def where(h, block):
        g, q = block // half, block % half
        q = q if g % 2 == 0 else half - 1 - q
        return (h * half + q) * groups + g

    steps = [(h, block) for h in range(2) for block in range(groups * half - 1)]
    down = [(where(h, block), where(h, block + 1)) for h, block in steps]
    above = lax.ppermute(bottom, ("ka", "row"), down)
    below = lax.ppermute(top, ("ka", "row"), [(j, i) for i, j in down])
    pieces = inner(b, t, (top, bottom, above, below), n, kl, rb, rest)
    out = join(exchange(pieces), n, rows, rb)
    return out.reshape(DEPTH // n, rows, cols)


def solution(mesh):
    in_specs = (P(None, "ka", "row", None),)
    out_specs = P("ka", "row", None)
    return jax.shard_map(body, mesh=mesh, in_specs=in_specs, out_specs=out_specs, check_vma=False)
```

```python
import functools
import math

import jax
import jax.numpy as jnp
import numpy as np
from jax import lax
from jax.experimental import pallas as pl
from jax.experimental.pallas import tpu as pltpu
from jax.sharding import PartitionSpec as P

K = 1024
DEPTH = 512
LANES = 128
EDGE = 16
F32 = jnp.float32
BF16 = jnp.bfloat16


def table():
    phase = (np.arange(K)[None, :] * np.arange(DEPTH)[:, None]) % K
    angle = phase.astype(np.float32) * np.float32(2.0 * math.pi / K)
    both = np.concatenate([np.cos(angle), np.sin(angle)], axis=0)
    return both.astype(jnp.bfloat16)


def place(dest, half, rb, mirrored):
    h = dest // half
    q = dest % half
    q = jnp.where(mirrored, half - 1 - q, q)
    return h, q * rb


def params(mib=48):
    return pltpu.CompilerParams(vmem_limit_bytes=mib * 1024 * 1024)


def split_kernel(n, rows, kl, rb, first, rest, x_ref, *refs):
    half = n // 2
    a_refs, b_refs, x32 = refs[:n], refs[n:-1], refs[-1]
    me = lax.axis_index("ka")
    mirrored = lax.axis_index("row") % 2 == 1
    x32[0] = x_ref[:, :LANES].astype(F32)
    x32[1] = x_ref[:, LANES:].astype(F32)
    lane = lax.broadcasted_iota(jnp.int32, (kl, LANES), 1)
    edges = [jnp.zeros((kl, LANES), F32) for _ in range(n * EDGE // LANES)]
    for s in range(n):
        h, row = place(me ^ s, half, rb, mirrored)
        for refs_of, group in ((a_refs, first), (b_refs, rest)):
            for slot, j in enumerate(group):
                for p in range(2):
                    y = x32[h, pl.ds(p * kl * rows + row + j, kl, stride=rows), :]
                    refs_of[s][pl.ds((slot * 2 + p) * kl, kl), :] = y.astype(BF16)
                    at, m = divmod(s * EDGE + p * 8 + 1 + j, LANES)[::-1]
                    y = pltpu.roll(y, (at + 1 - h) % LANES, 1)
                    edges[m] = jnp.where(lane == at, y, edges[m])
    for m, e in enumerate(edges):
        if kl < LANES:
            e = jnp.concatenate([e, jnp.zeros((LANES - kl, LANES), F32)], axis=0)
        e = e.T.astype(BF16)
        for i in range(LANES // EDGE):
            s = (m * LANES // EDGE + i) ^ half
            a_refs[s][pl.ds(len(first) * 2 * kl, EDGE), :] = e[i * EDGE : (i + 1) * EDGE]


def split(x, n, rows, kl, rb, first, rest):
    a_shape = jax.ShapeDtypeStruct((len(first) * 2 * kl + EDGE, LANES), BF16)
    b_shape = jax.ShapeDtypeStruct((len(rest) * 2 * kl, LANES), BF16)
    out = pl.pallas_call(
        functools.partial(split_kernel, n, rows, kl, rb, first, rest),
        out_shape=[a_shape] * n + ([b_shape] * n if rest else []),
        scratch_shapes=[pltpu.VMEM((2, 2 * kl * rows, LANES), F32)],
        compiler_params=params(),
        cost_estimate=pl.CostEstimate(flops=10**6, bytes_accessed=4 * 2**20, transcendentals=0),
        name="split",
    )(x)
    return out[:n], out[n:]


def transform(t_ref, pieces, kl, slot):
    n = len(pieces)
    me = lax.axis_index("ka")
    t = jnp.concatenate([t_ref[me ^ s] for s in range(n)], axis=1)
    x = jnp.concatenate(
        [
            jnp.concatenate([p[pl.ds((slot * 2 + q) * kl, kl), :] for p in pieces], axis=0)
            for q in range(2)
        ],
        axis=1,
    )
    return rounded(jnp.dot(t, x, preferred_element_type=F32))


def rounded(x):
    return (x * (float(K) ** -0.5)).astype(BF16)


def terms(a1, b1, a2, b2):
    re = a1 * a2 + b1 * b2
    im = b1 * a2 - a1 * b2
    pw = (a1 * a1 + b1 * b1 + a2 * a2 + b2 * b2) * 0.5
    return re, im, pw


def outer_kernel(n, kl, first, *refs):
    pieces, t_ref, outs = refs[:n], refs[n], refs[n + 1 :]
    for slot in range(len(first)):
        s = transform(t_ref, pieces, kl, slot)
        outs[slot][: 2 * DEPTH, :] = s[:, :LANES]
        outs[slot][2 * DEPTH : 4 * DEPTH, :] = s[:, LANES:]
    me = lax.axis_index("ka")
    t = jnp.concatenate([t_ref[me ^ s] for s in range(n)], axis=1)
    e = jnp.concatenate([p[len(first) * 2 * kl :, :kl] for p in pieces], axis=1)
    e = jnp.concatenate([e, jnp.zeros((LANES - EDGE, K), BF16)], axis=0)
    se = lax.dot_general(t, e, (((1,), (1,)), ((), ())), preferred_element_type=F32)
    se = rounded(se).astype(F32)
    packed = se[:LANES]
    for b in range(1, 2 * DEPTH // LANES):
        packed = packed + pltpu.roll(se[b * LANES : (b + 1) * LANES], EDGE * b, 1)
    packed = packed.astype(BF16)
    for slot in range(len(first)):
        outs[slot][4 * DEPTH :, :] = packed


def outer(pieces, t, n, kl, first):
    return pl.pallas_call(
        functools.partial(outer_kernel, n, kl, first),
        out_shape=[jax.ShapeDtypeStruct((4 * DEPTH + LANES, LANES), BF16)] * len(first),
        compiler_params=params(),
        cost_estimate=pl.CostEstimate(
            flops=2 * 2 * DEPTH * K * 256 * 3, bytes_accessed=4 * 2**20, transcendentals=0
        ),
        name="outer",
    )(*pieces, t)


def inner_kernel(n, kl, rest, *refs):
    pieces, t_ref, out = refs[:n], refs[n], refs[n + 1]
    for slot in range(len(rest)):
        s = transform(t_ref, pieces, kl, slot)
        out[slot, : 2 * DEPTH, :] = s[:, :LANES]
        out[slot, 2 * DEPTH :, :] = s[:, LANES:]


def inner(pieces, t, n, kl, rest):
    return pl.pallas_call(
        functools.partial(inner_kernel, n, kl, rest),
        out_shape=jax.ShapeDtypeStruct((len(rest), 4 * DEPTH, LANES), BF16),
        compiler_params=params(),
        cost_estimate=pl.CostEstimate(flops=3 * 10**10, bytes_accessed=6 * 2**20, transcendentals=0),
        name="inner",
    )(*pieces, t)


STEP = 16


def box_kernel(n, rb, *refs):
    above, top = refs[0], refs[1]
    inside = refs[2] if rb > 2 else None
    bottom, below = refs[2 + (rb > 2)], refs[3 + (rb > 2)]
    outs = refs[4 + (rb > 2) :][:n]
    edge, total, dec = refs[-3:]
    me = lax.axis_index("ka")
    h = me // (n // 2)
    dl = DEPTH // n

    def spectrum(r, z):
        ref = {-1: above, 0: top, rb - 1: bottom, rb: below}.get(r)
        where = [pl.ds(z + j * DEPTH, STEP) for j in range(4)]
        rows = [ref[w, :] for w in where] if ref is not None else [inside[r - 1, w, :] for w in where]
        return [x.astype(F32) for x in rows]

    lane = lax.broadcasted_iota(jnp.int32, (LANES, LANES), 1)
    packed = top[4 * DEPTH :, :].astype(F32)
    up = pltpu.roll(above[4 * DEPTH :, :].astype(F32), LANES - rb, 1)
    down = pltpu.roll(below[4 * DEPTH :, :].astype(F32), rb, 1)
    packed = jnp.where(lane % 8 == 0, up, jnp.where(lane % 8 == rb + 1, down, packed))
    blocks = DEPTH // LANES
    for b in range(blocks):
        c = packed if b == 0 else pltpu.roll(packed, LANES - EDGE * b, 1)
        s = pltpu.roll(packed, LANES - EDGE * (b + blocks), 1)
        c2, s2 = pltpu.roll(c, LANES - 8, 1), pltpu.roll(s, LANES - 8, 1)
        for t, v in enumerate(terms(c, s, c2, s2)):
            v = v + pltpu.roll(v, 1, 1) + pltpu.roll(v, LANES - 1, 1)
            edge[t, pl.ds(b * LANES + 8, LANES), :] = v
    for t in range(3):
        for z in (0, DEPTH + 8):
            edge[t, pl.ds(z, 8), :] = jnp.zeros((8, LANES), F32)
            for r in range(rb):
                total[r, t, pl.ds(z, 8), :] = jnp.zeros((8, LANES), F32)

    @pl.loop(0, DEPTH // STEP, unroll=2)
    def _(i):
        z = pl.multiple_of(i * STEP, STEP)
        before = terms(*spectrum(-1, z))
        here = terms(*spectrum(0, z))
        pair = [x + y for x, y in zip(before, here)]
        for r in range(rb):
            after = terms(*spectrum(r + 1, z))
            for t in range(3):
                total[r, t, pl.ds(z + 8, STEP), :] = pair[t] + after[t]
            pair = [x + y for x, y in zip(here, after)]
            here = after

    lane = lax.broadcasted_iota(jnp.int32, (STEP, LANES), 1)
    not_first, not_last = lane > 0, lane < LANES - 1
    at_edge = lane == jnp.where(h == 0, LANES - 1, 0)

    def deep(x):
        return x[0] + x[1] + x[2]

    @pl.loop(0, DEPTH // STEP)
    def _(i):
        z = pl.multiple_of(i * STEP, STEP)
        rim = [deep([edge[t, pl.ds(z + j, STEP), :] for j in (7, 8, 9)]) for t in range(3)]
        for r in range(rb):
            box = []
            for t in range(3):
                v = deep([total[r, t, pl.ds(z + j, STEP), :] for j in (7, 8, 9)])
                left = jnp.where(not_first, pltpu.roll(v, 1, 1), 0.0)
                right = jnp.where(not_last, pltpu.roll(v, LANES - 1, 1), 0.0)
                e = jnp.where(at_edge, pltpu.roll(rim[t], LANES - 2 - r + h, 1), 0.0)
                box.append(v + left + right + e)
            square = box[0] * box[0] + box[1] * box[1]
            d = 1.0 - jnp.sqrt(square) / (box[2] + 1e-05)
            dec[r, pl.ds(z, STEP), :] = (d * jnp.abs(d) * (d * d)).astype(BF16)

    for s in range(n):
        z = pl.multiple_of((me ^ s) * dl, dl)
        for r in range(rb):
            outs[s][pl.ds(r * dl, dl), :] = dec[r, pl.ds(z, dl), :]


def boxed(rows, n, rb):
    return pl.pallas_call(
        functools.partial(box_kernel, n, rb),
        out_shape=[jax.ShapeDtypeStruct((rb * (DEPTH // n), LANES), BF16)] * n,
        scratch_shapes=[
            pltpu.VMEM((3, DEPTH + 16, LANES), F32),
            pltpu.VMEM((rb, 3, DEPTH + 16, LANES), F32),
            pltpu.VMEM((rb, DEPTH, LANES), BF16),
        ],
        compiler_params=params(),
        cost_estimate=pl.CostEstimate(flops=10**7, bytes_accessed=6 * 2**20, transcendentals=0),
        name="boxed",
    )(*rows)


def join_kernel(n, rows, rb, *refs):
    half = n // 2
    pieces, out, held = refs[:n], refs[n], refs[n + 1]
    me = lax.axis_index("ka")
    mirrored = lax.axis_index("row") % 2 == 1
    dl = DEPTH // n
    for s in range(n):
        h, row = place(me ^ s, half, rb, mirrored)
        for r in range(rb):
            coded = pieces[s][pl.ds(r * dl, dl), :].astype(F32)
            d = jnp.sqrt(jnp.sqrt(jnp.abs(coded)))
            d = jnp.where(coded < 0.0, -d, d)
            held[h, pl.ds(row + r, dl, stride=rows), :] = d
    out[:, :LANES] = held[0]
    out[:, LANES:] = held[1]


def join(pieces, n, rows, rb):
    return pl.pallas_call(
        functools.partial(join_kernel, n, rows, rb),
        out_shape=jax.ShapeDtypeStruct((DEPTH // n * rows, 2 * LANES), F32),
        scratch_shapes=[pltpu.VMEM((2, DEPTH // n * rows, LANES), F32)],
        compiler_params=params(),
        cost_estimate=pl.CostEstimate(flops=10**6, bytes_accessed=2 * 2**20, transcendentals=0),
        name="join",
    )(*pieces)


def body(frames):
    n, groups = lax.axis_size("ka"), lax.axis_size("row")
    _, kl, rows, cols = frames.shape
    half = n // 2
    rb = rows // half
    first, rest = (0, rb - 1), tuple(range(1, rb - 1))
    t = jnp.asarray(table().reshape(2 * DEPTH, n, kl).transpose(1, 0, 2))

    order = sorted(range(1, n), key=lambda s: (s & half) == 0)

    def exchange(pieces):
        out = list(pieces)
        for s in order:
            out[s] = lax.ppermute(pieces[s], "ka", [(i, i ^ s) for i in range(n)])
        return out

    a, b = split(frames.reshape(2 * kl * rows, cols), n, rows, kl, rb, first, rest)
    a = exchange(a)
    b = exchange(b) if rest else []
    top, bottom = outer(a, t, n, kl, first)

    def where(h, block):
        g, q = block // half, block % half
        q = q if g % 2 == 0 else half - 1 - q
        return (h * half + q) * groups + g

    steps = [(h, block) for h in range(2) for block in range(groups * half - 1)]
    down = [(where(h, block), where(h, block + 1)) for h, block in steps]
    above = lax.ppermute(bottom, ("ka", "row"), down)
    below = lax.ppermute(top, ("ka", "row"), [(j, i) for i, j in down])
    inside = [inner(b, t, n, kl, rest)] if rest else []
    pieces = boxed([above, top, *inside, bottom, below], n, rb)
    out = join(exchange(pieces), n, rows, rb)
    return out.reshape(DEPTH // n, rows, cols)


def solution(mesh):
    in_specs = (P(None, "ka", "row", None),)
    out_specs = P("ka", "row", None)
    return jax.shard_map(body, mesh=mesh, in_specs=in_specs, out_specs=out_specs, check_vma=False)
```

```python
import functools
import math

import jax
import jax.numpy as jnp
import numpy as np
from jax import lax
from jax.experimental import pallas as pl
from jax.experimental.pallas import tpu as pltpu
from jax.sharding import PartitionSpec as P

K = 1024
DEPTH = 512
LANES = 128
AFTER = 2
EDGE = 16
F32 = jnp.float32
BF16 = jnp.bfloat16


def table():
    phase = (np.arange(K)[None, :] * np.arange(DEPTH)[:, None]) % K
    angle = phase.astype(np.float32) * np.float32(2.0 * math.pi / K)
    both = np.concatenate([np.cos(angle), np.sin(angle)], axis=0)
    return both.astype(jnp.bfloat16)


def place(dest, half, rb, mirrored):
    h = dest // half
    q = dest % half
    q = jnp.where(mirrored, half - 1 - q, q)
    return h, q * rb


def params(mib=48):
    return pltpu.CompilerParams(vmem_limit_bytes=mib * 1024 * 1024)


def split_kernel(n, rows, kl, rb, group, edge, x_ref, *refs):
    half = n // 2
    outs, x32 = refs[-n - 1 : -1], refs[-1]
    me = lax.axis_index("ka")
    mirrored = lax.axis_index("row") % 2 == 1
    x32[0] = x_ref[:, :LANES].astype(F32)
    x32[1] = x_ref[:, LANES:].astype(F32)
    lane = lax.broadcasted_iota(jnp.int32, (kl, LANES), 1)
    edges = [jnp.zeros((kl, LANES), F32) for _ in range(n * EDGE // LANES)]
    for s in range(n):
        h, row = place(me ^ s, half, rb, mirrored)
        for j in range(rb) if edge else group:
            for p in range(2):
                y = x32[h, pl.ds(p * kl * rows + row + j, kl, stride=rows), :]
                if j in group:
                    slot = group.index(j)
                    outs[s][pl.ds((slot * 2 + p) * kl, kl), :] = y.astype(BF16)
                if edge:
                    m, at = divmod(s * EDGE + p * 8 + 1 + j, LANES)
                    y = pltpu.roll(y, (at + 1 - h) % LANES, 1)
                    edges[m] = jnp.where(lane == at, y, edges[m])
    for m, e in enumerate(edges if edge else []):
        if kl < LANES:
            e = jnp.concatenate([e, jnp.zeros((LANES - kl, LANES), F32)], axis=0)
        e = e.T.astype(BF16)
        for i in range(LANES // EDGE):
            s = (m * LANES // EDGE + i) ^ half
            outs[s][pl.ds(len(group) * 2 * kl, EDGE), :] = e[i * EDGE : (i + 1) * EDGE]


def split(x, n, rows, kl, rb, group, edge, after=()):
    size = len(group) * 2 * kl + (EDGE if edge else 0)
    return pl.pallas_call(
        functools.partial(split_kernel, n, rows, kl, rb, group, edge),
        out_shape=[jax.ShapeDtypeStruct((size, LANES), BF16)] * n,
        in_specs=[pl.BlockSpec(memory_space=pltpu.VMEM)]
        + [pl.BlockSpec(memory_space=pl.ANY)] * len(after),
        scratch_shapes=[pltpu.VMEM((2, 2 * kl * rows, LANES), F32)],
        compiler_params=params(),
        cost_estimate=pl.CostEstimate(flops=10**6, bytes_accessed=4 * 2**20, transcendentals=0),
        name="split",
    )(x, *after)


def transform(t_ref, pieces, kl, slot):
    n = len(pieces)
    me = lax.axis_index("ka")
    t = jnp.concatenate([t_ref[me ^ s] for s in range(n)], axis=1)
    x = jnp.concatenate(
        [
            jnp.concatenate([p[pl.ds((slot * 2 + q) * kl, kl), :] for p in pieces], axis=0)
            for q in range(2)
        ],
        axis=1,
    )
    return rounded(jnp.dot(t, x, preferred_element_type=F32))


def rounded(x):
    return (x * (float(K) ** -0.5)).astype(BF16)


def terms(a1, b1, a2, b2):
    re = a1 * a2 + b1 * b2
    im = b1 * a2 - a1 * b2
    pw = (a1 * a1 + b1 * b1 + a2 * a2 + b2 * b2) * 0.5
    return re, im, pw


def outer_kernel(n, kl, first, *refs):
    pieces, t_ref, outs = refs[:n], refs[n], refs[n + 1 :]
    for slot in range(len(first)):
        s = transform(t_ref, pieces, kl, slot)
        outs[slot][: 2 * DEPTH, :] = s[:, :LANES]
        outs[slot][2 * DEPTH : 4 * DEPTH, :] = s[:, LANES:]
    me = lax.axis_index("ka")
    t = jnp.concatenate([t_ref[me ^ s] for s in range(n)], axis=1)
    e = jnp.concatenate([p[len(first) * 2 * kl :, :kl] for p in pieces], axis=1)
    e = jnp.concatenate([e, jnp.zeros((LANES - EDGE, K), BF16)], axis=0)
    se = lax.dot_general(t, e, (((1,), (1,)), ((), ())), preferred_element_type=F32)
    se = rounded(se).astype(F32)
    packed = se[:LANES]
    for b in range(1, 2 * DEPTH // LANES):
        packed = packed + pltpu.roll(se[b * LANES : (b + 1) * LANES], EDGE * b, 1)
    packed = packed.astype(BF16)
    for slot in range(len(first)):
        outs[slot][4 * DEPTH :, :] = packed


def outer(pieces, t, n, kl, first):
    return pl.pallas_call(
        functools.partial(outer_kernel, n, kl, first),
        out_shape=[jax.ShapeDtypeStruct((4 * DEPTH + LANES, LANES), BF16)] * len(first),
        compiler_params=params(),
        cost_estimate=pl.CostEstimate(
            flops=2 * 2 * DEPTH * K * 256 * 3, bytes_accessed=4 * 2**20, transcendentals=0
        ),
        name="outer",
    )(*pieces, t)


def inner_kernel(n, kl, rest, *refs):
    pieces, t_ref, out = refs[:n], refs[n], refs[n + 1]
    for slot in range(len(rest)):
        s = transform(t_ref, pieces, kl, slot)
        out[slot, : 2 * DEPTH, :] = s[:, :LANES]
        out[slot, 2 * DEPTH :, :] = s[:, LANES:]


def inner(pieces, t, n, kl, rest):
    return pl.pallas_call(
        functools.partial(inner_kernel, n, kl, rest),
        out_shape=jax.ShapeDtypeStruct((len(rest), 4 * DEPTH, LANES), BF16),
        compiler_params=params(),
        cost_estimate=pl.CostEstimate(flops=4 * 10**9, bytes_accessed=6 * 2**20, transcendentals=0),
        name="inner",
    )(*pieces, t)


STEP = 16


def box_kernel(n, rb, *refs):
    above, top = refs[0], refs[1]
    inside = refs[2] if rb > 2 else None
    bottom, below = refs[2 + (rb > 2)], refs[3 + (rb > 2)]
    outs = refs[4 + (rb > 2) :][:n]
    edge, total, dec = refs[-3:]
    me = lax.axis_index("ka")
    h = me // (n // 2)
    dl = DEPTH // n

    def spectrum(r, z):
        ref = {-1: above, 0: top, rb - 1: bottom, rb: below}.get(r)
        where = [pl.ds(z + j * DEPTH, STEP) for j in range(4)]
        rows = [ref[w, :] for w in where] if ref is not None else [inside[r - 1, w, :] for w in where]
        return [x.astype(F32) for x in rows]

    lane = lax.broadcasted_iota(jnp.int32, (LANES, LANES), 1)
    packed = top[4 * DEPTH :, :].astype(F32)
    up = pltpu.roll(above[4 * DEPTH :, :].astype(F32), LANES - rb, 1)
    down = pltpu.roll(below[4 * DEPTH :, :].astype(F32), rb, 1)
    packed = jnp.where(lane % 8 == 0, up, jnp.where(lane % 8 == rb + 1, down, packed))
    blocks = DEPTH // LANES
    for b in range(blocks):
        c = packed if b == 0 else pltpu.roll(packed, LANES - EDGE * b, 1)
        s = pltpu.roll(packed, LANES - EDGE * (b + blocks), 1)
        c2, s2 = pltpu.roll(c, LANES - 8, 1), pltpu.roll(s, LANES - 8, 1)
        for t, v in enumerate(terms(c, s, c2, s2)):
            v = v + pltpu.roll(v, 1, 1) + pltpu.roll(v, LANES - 1, 1)
            edge[t, pl.ds(b * LANES + 8, LANES), :] = v
    for t in range(3):
        for z in (0, DEPTH + 8):
            edge[t, pl.ds(z, 8), :] = jnp.zeros((8, LANES), F32)
            for r in range(rb):
                total[r, t, pl.ds(z, 8), :] = jnp.zeros((8, LANES), F32)

    @pl.loop(0, DEPTH // STEP, unroll=2)
    def _(i):
        z = pl.multiple_of(i * STEP, STEP)
        before = terms(*spectrum(-1, z))
        here = terms(*spectrum(0, z))
        pair = [x + y for x, y in zip(before, here)]
        for r in range(rb):
            after = terms(*spectrum(r + 1, z))
            for t in range(3):
                total[r, t, pl.ds(z + 8, STEP), :] = pair[t] + after[t]
            pair = [x + y for x, y in zip(here, after)]
            here = after

    lane = lax.broadcasted_iota(jnp.int32, (STEP, LANES), 1)
    not_first, not_last = lane > 0, lane < LANES - 1
    at_edge = lane == jnp.where(h == 0, LANES - 1, 0)

    def deep(x):
        return x[0] + x[1] + x[2]

    @pl.loop(0, DEPTH // STEP, unroll=4)
    def _(i):
        z = pl.multiple_of(i * STEP, STEP)
        rim = [deep([edge[t, pl.ds(z + j, STEP), :] for j in (7, 8, 9)]) for t in range(3)]
        for r in range(rb):
            box = []
            for t in range(3):
                v = deep([total[r, t, pl.ds(z + j, STEP), :] for j in (7, 8, 9)])
                left = jnp.where(not_first, pltpu.roll(v, 1, 1), 0.0)
                right = jnp.where(not_last, pltpu.roll(v, LANES - 1, 1), 0.0)
                e = jnp.where(at_edge, pltpu.roll(rim[t], LANES - 2 - r + h, 1), 0.0)
                box.append(v + left + right + e)
            square = box[0] * box[0] + box[1] * box[1]
            d = 1.0 - jnp.sqrt(square) / (box[2] + 1e-05)
            dec[r, pl.ds(z, STEP), :] = (d * jnp.abs(d) * (d * d)).astype(BF16)

    for s in range(n):
        z = pl.multiple_of((me ^ s) * dl, dl)
        for r in range(rb):
            outs[s][pl.ds(r * dl, dl), :] = dec[r, pl.ds(z, dl), :]


def boxed(rows, n, rb):
    return pl.pallas_call(
        functools.partial(box_kernel, n, rb),
        out_shape=[jax.ShapeDtypeStruct((rb * (DEPTH // n), LANES), BF16)] * n,
        scratch_shapes=[
            pltpu.VMEM((3, DEPTH + 16, LANES), F32),
            pltpu.VMEM((rb, 3, DEPTH + 16, LANES), F32),
            pltpu.VMEM((rb, DEPTH, LANES), BF16),
        ],
        compiler_params=params(),
        cost_estimate=pl.CostEstimate(flops=10**7, bytes_accessed=6 * 2**20, transcendentals=0),
        name="boxed",
    )(*rows)


def join_kernel(n, rows, rb, *refs):
    half = n // 2
    pieces, out, held = refs[:n], refs[n], refs[n + 1]
    me = lax.axis_index("ka")
    mirrored = lax.axis_index("row") % 2 == 1
    dl = DEPTH // n
    for s in range(n):
        h, row = place(me ^ s, half, rb, mirrored)
        for r in range(rb):
            coded = pieces[s][pl.ds(r * dl, dl), :].astype(F32)
            d = jnp.sqrt(jnp.sqrt(jnp.abs(coded)))
            d = jnp.where(coded < 0.0, -d, d)
            held[h, pl.ds(row + r, dl, stride=rows), :] = d
    out[:, :LANES] = held[0]
    out[:, LANES:] = held[1]


def join(pieces, n, rows, rb):
    return pl.pallas_call(
        functools.partial(join_kernel, n, rows, rb),
        out_shape=jax.ShapeDtypeStruct((DEPTH // n * rows, 2 * LANES), F32),
        scratch_shapes=[pltpu.VMEM((2, DEPTH // n * rows, LANES), F32)],
        compiler_params=params(),
        cost_estimate=pl.CostEstimate(flops=10**6, bytes_accessed=2 * 2**20, transcendentals=0),
        name="join",
    )(*pieces)


def body(frames):
    n, groups = lax.axis_size("ka"), lax.axis_size("row")
    _, kl, rows, cols = frames.shape
    half = n // 2
    rb = rows // half
    first, rest = (0, rb - 1), tuple(range(1, rb - 1))
    t = jnp.asarray(table().reshape(2 * DEPTH, n, kl).transpose(1, 0, 2))

    far, near, core = range(half, n), range(2, half), range(1, 2)

    def exchange(pieces, order):
        out = list(pieces)
        for s in order:
            out[s] = lax.ppermute(pieces[s], "ka", [(i, i ^ s) for i in range(n)])
        return out

    x = frames.reshape(2 * kl * rows, cols)
    a = exchange(split(x, n, rows, kl, rb, first, True), [*far, *near, *core])
    b = []
    if rest:
        b = exchange(split(x, n, rows, kl, rb, rest, False, [a[[*far, *near, *core][AFTER]]]), [*far, *near, *core])
    top, bottom = outer(a, t, n, kl, first)

    def where(h, block):
        g, q = block // half, block % half
        q = q if g % 2 == 0 else half - 1 - q
        return (h * half + q) * groups + g

    steps = [(h, block) for h in range(2) for block in range(groups * half - 1)]
    down = [(where(h, block), where(h, block + 1)) for h, block in steps]
    above = lax.ppermute(bottom, ("ka", "row"), down)
    below = lax.ppermute(top, ("ka", "row"), [(j, i) for i, j in down])
    inside = [inner(b, t, n, kl, rest)] if rest else []
    pieces = boxed([above, top, *inside, bottom, below], n, rb)
    out = join(exchange(pieces, [*near, *far, *core]), n, rows, rb)
    return out.reshape(DEPTH // n, rows, cols)


def solution(mesh):
    in_specs = (P(None, "ka", "row", None),)
    out_specs = P("ka", "row", None)
    return jax.shard_map(body, mesh=mesh, in_specs=in_specs, out_specs=out_specs, check_vma=False)
```

```python
import functools
import math

import jax
import jax.numpy as jnp
import numpy as np
from jax import lax
from jax.experimental import pallas as pl
from jax.experimental.pallas import tpu as pltpu
from jax.sharding import PartitionSpec as P

K = 1024
DEPTH = 512
LANES = 128
AFTER = 2
EDGE = 16
F32 = jnp.float32
BF16 = jnp.bfloat16


def table():
    phase = (np.arange(K)[None, :] * np.arange(DEPTH)[:, None]) % K
    angle = phase.astype(np.float32) * np.float32(2.0 * math.pi / K)
    both = np.concatenate([np.cos(angle), np.sin(angle)], axis=0)
    return both.astype(jnp.bfloat16)


def place(dest, half, rb, mirrored):
    h = dest // half
    q = dest % half
    q = jnp.where(mirrored, half - 1 - q, q)
    return h, q * rb


def params(mib=48):
    return pltpu.CompilerParams(vmem_limit_bytes=mib * 1024 * 1024)


def split_kernel(n, rows, kl, rb, group, edge, x_ref, *refs):
    half = n // 2
    outs, held, x32, sem = refs[-n - 3 : -3], refs[-3], refs[-2], refs[-1]
    me = lax.axis_index("ka")
    mirrored = lax.axis_index("row") % 2 == 1
    size = kl * rows
    copies = [
        pltpu.make_async_copy(x_ref.at[pl.ds(p * size, size)], held.at[p], sem.at[p])
        for p in range(2)
    ]
    for c in copies:
        c.start()
    lane = lax.broadcasted_iota(jnp.int32, (kl, LANES), 1)
    edges = [jnp.zeros((kl, LANES), F32) for _ in range(n * EDGE // LANES)]
    for p in range(2):
        copies[p].wait()
        for h in range(2):
            x32[p, h] = held[p, :, h * LANES : (h + 1) * LANES].astype(F32)
        for s in range(n):
            h, row = place(me ^ s, half, rb, mirrored)
            for j in range(rb) if edge else group:
                y = x32[p, h, pl.ds(row + j, kl, stride=rows), :]
                if j in group:
                    slot = group.index(j)
                    outs[s][pl.ds((slot * 2 + p) * kl, kl), :] = y.astype(BF16)
                if edge:
                    m, at = divmod(s * EDGE + p * 8 + 1 + j, LANES)
                    y = pltpu.roll(y, (at + 1 - h) % LANES, 1)
                    edges[m] = jnp.where(lane == at, y, edges[m])
    for m, e in enumerate(edges if edge else []):
        if kl < LANES:
            e = jnp.concatenate([e, jnp.zeros((LANES - kl, LANES), F32)], axis=0)
        e = e.T.astype(BF16)
        for i in range(LANES // EDGE):
            s = (m * LANES // EDGE + i) ^ half
            outs[s][pl.ds(len(group) * 2 * kl, EDGE), :] = e[i * EDGE : (i + 1) * EDGE]


def split(x, n, rows, kl, rb, group, edge, after=()):
    size = len(group) * 2 * kl + (EDGE if edge else 0)
    return pl.pallas_call(
        functools.partial(split_kernel, n, rows, kl, rb, group, edge),
        out_shape=[jax.ShapeDtypeStruct((size, LANES), BF16)] * n,
        in_specs=[pl.BlockSpec(memory_space=pltpu.HBM)]
        + [pl.BlockSpec(memory_space=pl.ANY)] * len(after),
        scratch_shapes=[
            pltpu.VMEM((2, kl * rows, 2 * LANES), BF16),
            pltpu.VMEM((2, 2, kl * rows, LANES), F32),
            pltpu.SemaphoreType.DMA((2,)),
        ],
        compiler_params=params(),
        cost_estimate=pl.CostEstimate(flops=10**6, bytes_accessed=4 * 2**20, transcendentals=0),
        name="split",
    )(x, *after)


def transform(t_ref, pieces, kl, slot):
    n = len(pieces)
    me = lax.axis_index("ka")
    t = jnp.concatenate([t_ref[me ^ s] for s in range(n)], axis=1)
    x = jnp.concatenate(
        [
            jnp.concatenate([p[pl.ds((slot * 2 + q) * kl, kl), :] for p in pieces], axis=0)
            for q in range(2)
        ],
        axis=1,
    )
    return rounded(jnp.dot(t, x, preferred_element_type=F32))


def rounded(x):
    return (x * (float(K) ** -0.5)).astype(BF16)


def terms(a1, b1, a2, b2):
    re = a1 * a2 + b1 * b2
    im = b1 * a2 - a1 * b2
    pw = (a1 * a1 + b1 * b1 + a2 * a2 + b2 * b2) * 0.5
    return re, im, pw


def outer_kernel(n, kl, first, *refs):
    pieces, t_ref, outs = refs[:n], refs[n], refs[n + 1 :]
    for slot in range(len(first)):
        s = transform(t_ref, pieces, kl, slot)
        outs[slot][: 2 * DEPTH, :] = s[:, :LANES]
        outs[slot][2 * DEPTH : 4 * DEPTH, :] = s[:, LANES:]
    me = lax.axis_index("ka")
    t = jnp.concatenate([t_ref[me ^ s] for s in range(n)], axis=1)
    e = jnp.concatenate([p[len(first) * 2 * kl :, :kl] for p in pieces], axis=1)
    e = jnp.concatenate([e, jnp.zeros((LANES - EDGE, K), BF16)], axis=0)
    se = lax.dot_general(t, e, (((1,), (1,)), ((), ())), preferred_element_type=F32)
    se = rounded(se).astype(F32)
    packed = se[:LANES]
    for b in range(1, 2 * DEPTH // LANES):
        packed = packed + pltpu.roll(se[b * LANES : (b + 1) * LANES], EDGE * b, 1)
    packed = packed.astype(BF16)
    for slot in range(len(first)):
        outs[slot][4 * DEPTH :, :] = packed


def outer(pieces, t, n, kl, first):
    return pl.pallas_call(
        functools.partial(outer_kernel, n, kl, first),
        out_shape=[jax.ShapeDtypeStruct((4 * DEPTH + LANES, LANES), BF16)] * len(first),
        compiler_params=params(),
        cost_estimate=pl.CostEstimate(
            flops=2 * 2 * DEPTH * K * 256 * 3, bytes_accessed=4 * 2**20, transcendentals=0
        ),
        name="outer",
    )(*pieces, t)


def inner_kernel(n, kl, rest, *refs):
    pieces, t_ref, out = refs[:n], refs[n], refs[n + 1]
    for slot in range(len(rest)):
        s = transform(t_ref, pieces, kl, slot)
        out[slot, : 2 * DEPTH, :] = s[:, :LANES]
        out[slot, 2 * DEPTH :, :] = s[:, LANES:]


def inner(pieces, t, n, kl, rest):
    return pl.pallas_call(
        functools.partial(inner_kernel, n, kl, rest),
        out_shape=jax.ShapeDtypeStruct((len(rest), 4 * DEPTH, LANES), BF16),
        compiler_params=params(),
        cost_estimate=pl.CostEstimate(flops=4 * 10**9, bytes_accessed=6 * 2**20, transcendentals=0),
        name="inner",
    )(*pieces, t)


STEP = 16


def box_kernel(n, rb, far, *refs):
    half, span, count = n // 2, DEPTH // 2, 4 + (rb > 2)
    above, top, bottom, below = refs[0], refs[1], refs[count - 2], refs[count - 1]
    inside = refs[2]
    outs = refs[count : count + half] if far else refs[count + 1 : count + 1 + half]
    edge = refs[count + half] if far else refs[count]
    total, dec = refs[-2:]
    me = lax.axis_index("ka")
    h = me // half
    dl = DEPTH // n
    base = pl.multiple_of((1 - h if far else h) * span, span)

    def spectrum(r, z):
        ref = {-1: above, 0: top, rb - 1: bottom, rb: below}.get(r)
        where = [pl.ds(z + j * DEPTH, STEP) for j in range(4)]
        rows = [ref[w, :] for w in where] if ref is not None else [inside[r - 1, w, :] for w in where]
        return [x.astype(F32) for x in rows]

    def make_edge():
        lane = lax.broadcasted_iota(jnp.int32, (LANES, LANES), 1)
        packed = top[4 * DEPTH :, :].astype(F32)
        up = pltpu.roll(above[4 * DEPTH :, :].astype(F32), LANES - rb, 1)
        down = pltpu.roll(below[4 * DEPTH :, :].astype(F32), rb, 1)
        packed = jnp.where(lane % 8 == 0, up, jnp.where(lane % 8 == rb + 1, down, packed))
        blocks = DEPTH // LANES
        for b in range(blocks):
            c = packed if b == 0 else pltpu.roll(packed, LANES - EDGE * b, 1)
            s = pltpu.roll(packed, LANES - EDGE * (b + blocks), 1)
            c2, s2 = pltpu.roll(c, LANES - 8, 1), pltpu.roll(s, LANES - 8, 1)
            for t, v in enumerate(terms(c, s, c2, s2)):
                v = v + pltpu.roll(v, 1, 1) + pltpu.roll(v, LANES - 1, 1)
                edge[t, pl.ds(b * LANES + 8, LANES), :] = v
        for t in range(3):
            for z in (0, DEPTH + 8):
                edge[t, pl.ds(z, 8), :] = jnp.zeros((8, LANES), F32)

    if far:
        make_edge()

    def over_rows(z, at, keep=None):
        before = terms(*spectrum(-1, z))
        here = terms(*spectrum(0, z))
        pair = [x + y for x, y in zip(before, here)]
        for r in range(rb):
            after = terms(*spectrum(r + 1, z))
            for t in range(3):
                v = pair[t] + after[t]
                v = v if keep is None else jnp.where(keep, v, 0.0)
                total[r, t, pl.ds(at, STEP), :] = v
            pair = [x + y for x, y in zip(here, after)]
            here = after

    @pl.loop(0, span // STEP, unroll=4)
    def _(i):
        z = pl.multiple_of(i * STEP, STEP)
        over_rows(pl.multiple_of(base + z, STEP), pl.multiple_of(z + STEP, STEP))

    z = pl.multiple_of(jnp.maximum(base - STEP, 0), STEP)
    over_rows(z, 0, base > 0)
    z = pl.multiple_of(jnp.minimum(base + span, DEPTH - STEP), STEP)
    over_rows(z, span + STEP, base + span < DEPTH)

    lane = lax.broadcasted_iota(jnp.int32, (STEP, LANES), 1)
    not_first, not_last = lane > 0, lane < LANES - 1
    at_edge = lane == jnp.where(h == 0, LANES - 1, 0)

    def deep(x):
        return x[0] + x[1] + x[2]

    @pl.loop(0, span // STEP, unroll=8)
    def _(i):
        z = pl.multiple_of(i * STEP, STEP)
        rim = [deep([edge[t, pl.ds(base + z + j, STEP), :] for j in (7, 8, 9)]) for t in range(3)]
        for r in range(rb):
            box = []
            for t in range(3):
                v = deep([total[r, t, pl.ds(z + STEP + j, STEP), :] for j in (-1, 0, 1)])
                left = jnp.where(not_first, pltpu.roll(v, 1, 1), 0.0)
                right = jnp.where(not_last, pltpu.roll(v, LANES - 1, 1), 0.0)
                e = jnp.where(at_edge, pltpu.roll(rim[t], LANES - 2 - r + h, 1), 0.0)
                box.append(v + left + right + e)
            square = box[0] * box[0] + box[1] * box[1]
            floor = box[2] + 1e-05
            scaled = jnp.maximum(square, 1e-27) * (floor * floor)
            d = 1.0 - square * lax.rsqrt(scaled)
            dec[r, pl.ds(z, STEP), :] = (d * jnp.abs(d) * (d * d)).astype(BF16)

    for i in range(half):
        z = pl.multiple_of(((me ^ i) % half) * dl, dl)
        for r in range(rb):
            outs[i][pl.ds(r * dl, dl), :] = dec[r, pl.ds(z, dl), :]


def boxed(rows, n, rb, edge=None):
    far = edge is None
    return pl.pallas_call(
        functools.partial(box_kernel, n, rb, far),
        out_shape=[jax.ShapeDtypeStruct((rb * (DEPTH // n), LANES), BF16)] * (n // 2)
        + ([jax.ShapeDtypeStruct((3, DEPTH + 16, LANES), F32)] if far else []),
        scratch_shapes=[
            pltpu.VMEM((rb, 3, DEPTH // 2 + 2 * STEP, LANES), F32),
            pltpu.VMEM((rb, DEPTH // 2, LANES), BF16),
        ],
        compiler_params=params(),
        cost_estimate=pl.CostEstimate(flops=10**7, bytes_accessed=6 * 2**20, transcendentals=0),
        name="boxed",
    )(*rows, *([] if far else [edge]))


def join_kernel(n, rows, rb, far, *refs):
    half = n // 2
    pieces = refs[:half]
    me = lax.axis_index("ka")
    mirrored = lax.axis_index("row") % 2 == 1
    dl = DEPTH // n
    held = refs[-1]
    for i in range(half):
        _, row = place(me ^ i, half, rb, mirrored)
        for r in range(rb):
            coded = pieces[i][pl.ds(r * dl, dl), :].astype(F32)
            d = jnp.sqrt(jnp.sqrt(jnp.abs(coded)))
            d = jnp.where(coded < 0.0, -d, d)
            held[pl.ds(row + r, dl, stride=rows), :] = d
    if not far:
        other, out = refs[half], refs[half + 1]
        left = me < half
        out[:, :LANES] = jnp.where(left, held[...], other[...])
        out[:, LANES:] = jnp.where(left, other[...], held[...])


def join(pieces, n, rows, rb, other=None):
    far = other is None
    size = DEPTH // n * rows
    return pl.pallas_call(
        functools.partial(join_kernel, n, rows, rb, far),
        out_shape=jax.ShapeDtypeStruct((size, LANES if far else 2 * LANES), F32),
        scratch_shapes=[] if far else [pltpu.VMEM((size, LANES), F32)],
        compiler_params=params(),
        cost_estimate=pl.CostEstimate(
            flops=1 * 10**9 if far else 10**6, bytes_accessed=2 * 2**20, transcendentals=0
        ),
        name="join",
    )(*pieces, *([] if far else [other]))


def body(frames):
    n, groups = lax.axis_size("ka"), lax.axis_size("row")
    _, kl, rows, cols = frames.shape
    half = n // 2
    rb = rows // half
    first, rest = (0, rb - 1), tuple(range(1, rb - 1))
    t = jnp.asarray(table().reshape(2 * DEPTH, n, kl).transpose(1, 0, 2))

    far, near, core = range(half, n), range(2, half), range(1, 2)

    def exchange(pieces, order):
        out = list(pieces)
        for s in order:
            out[s] = lax.ppermute(pieces[s], "ka", [(i, i ^ s) for i in range(n)])
        return out

    x = pltpu.with_memory_space_constraint(frames.reshape(2 * kl * rows, cols), pltpu.HBM)
    a = exchange(split(x, n, rows, kl, rb, first, True), [*far, *near, *core])
    b = []
    if rest:
        b = exchange(split(x, n, rows, kl, rb, rest, False, [a[[*far, *near, *core][AFTER]]]), [*far, *near, *core])
    top, bottom = outer(a, t, n, kl, first)

    def where(h, block):
        g, q = block // half, block % half
        q = q if g % 2 == 0 else half - 1 - q
        return (h * half + q) * groups + g

    steps = [(h, block) for h in range(2) for block in range(groups * half - 1)]
    down = [(where(h, block), where(h, block + 1)) for h, block in steps]
    above = lax.ppermute(bottom, ("ka", "row"), down)
    below = lax.ppermute(top, ("ka", "row"), [(j, i) for i, j in down])
    inside = [inner(b, t, n, kl, rest)] if rest else []
    spectra = [above, top, *inside, bottom, below]
    *away, edge = boxed(spectra, n, rb)
    pieces = [*boxed(spectra, n, rb, edge), *away]
    pieces = exchange(pieces, [*far, *near, *core])
    out = join(pieces[:half], n, rows, rb, join(pieces[half:], n, rows, rb))
    return out.reshape(DEPTH // n, rows, cols)


def solution(mesh):
    in_specs = (P(None, "ka", "row", None),)
    out_specs = P("ka", "row", None)
    return jax.shard_map(body, mesh=mesh, in_specs=in_specs, out_specs=out_specs, check_vma=False)
```

```python
import functools
import math

import jax
import jax.numpy as jnp
import numpy as np
from jax import lax
from jax.experimental import pallas as pl
from jax.experimental.pallas import tpu as pltpu
from jax.sharding import PartitionSpec as P

K = 1024
DEPTH = 512
LANES = 128
AFTER = 2
EDGE = 16
F32 = jnp.float32
BF16 = jnp.bfloat16


def table():
    phase = (np.arange(K)[None, :] * np.arange(DEPTH)[:, None]) % K
    angle = phase.astype(np.float32) * np.float32(2.0 * math.pi / K)
    both = np.concatenate([np.cos(angle), np.sin(angle)], axis=0)
    return both.astype(jnp.bfloat16)


def place(dest, half, rb, mirrored):
    h = dest // half
    q = dest % half
    q = jnp.where(mirrored, half - 1 - q, q)
    return h, q * rb


def params(mib=48):
    return pltpu.CompilerParams(vmem_limit_bytes=mib * 1024 * 1024)


def split_kernel(n, rows, kl, rb, group, edge, x_ref, *refs):
    half = n // 2
    outs, held, x32, sem = refs[-n - 3 : -3], refs[-3], refs[-2], refs[-1]
    me = lax.axis_index("ka")
    mirrored = lax.axis_index("row") % 2 == 1
    size = kl * rows
    copies = [
        pltpu.make_async_copy(x_ref.at[pl.ds(p * size, size)], held.at[p], sem.at[p])
        for p in range(2)
    ]
    for c in copies:
        c.start()
    lane = lax.broadcasted_iota(jnp.int32, (kl, LANES), 1)
    edges = [jnp.zeros((kl, LANES), F32) for _ in range(n * EDGE // LANES)]
    for p in range(2):
        copies[p].wait()
        for h in range(2):
            x32[p, h] = held[p, :, h * LANES : (h + 1) * LANES].astype(F32)
        for s in range(n):
            h, row = place(me ^ s, half, rb, mirrored)
            for j in range(rb) if edge else group:
                y = x32[p, h, pl.ds(row + j, kl, stride=rows), :]
                if j in group:
                    slot = group.index(j)
                    outs[s][pl.ds((slot * 2 + p) * kl, kl), :] = y.astype(BF16)
                if edge:
                    m, at = divmod(s * EDGE + p * 8 + 1 + j, LANES)
                    y = pltpu.roll(y, (at + 1 - h) % LANES, 1)
                    edges[m] = jnp.where(lane == at, y, edges[m])
    for m, e in enumerate(edges if edge else []):
        if kl < LANES:
            e = jnp.concatenate([e, jnp.zeros((LANES - kl, LANES), F32)], axis=0)
        e = e.T.astype(BF16)
        for i in range(LANES // EDGE):
            s = (m * LANES // EDGE + i) ^ half
            outs[s][pl.ds(len(group) * 2 * kl, EDGE), :] = e[i * EDGE : (i + 1) * EDGE]


def split(x, n, rows, kl, rb, group, edge, after=()):
    size = len(group) * 2 * kl + (EDGE if edge else 0)
    return pl.pallas_call(
        functools.partial(split_kernel, n, rows, kl, rb, group, edge),
        out_shape=[jax.ShapeDtypeStruct((size, LANES), BF16)] * n,
        in_specs=[pl.BlockSpec(memory_space=pltpu.HBM)]
        + [pl.BlockSpec(memory_space=pl.ANY)] * len(after),
        scratch_shapes=[
            pltpu.VMEM((2, kl * rows, 2 * LANES), BF16),
            pltpu.VMEM((2, 2, kl * rows, LANES), F32),
            pltpu.SemaphoreType.DMA((2,)),
        ],
        compiler_params=params(),
        cost_estimate=pl.CostEstimate(flops=10**6, bytes_accessed=4 * 2**20, transcendentals=0),
        name="split",
    )(x, *after)


def transform(t_ref, pieces, kl, slot):
    n = len(pieces)
    me = lax.axis_index("ka")
    t = jnp.concatenate([t_ref[me ^ s] for s in range(n)], axis=1)
    x = jnp.concatenate(
        [
            jnp.concatenate([p[pl.ds((slot * 2 + q) * kl, kl), :] for p in pieces], axis=0)
            for q in range(2)
        ],
        axis=1,
    )
    return rounded(jnp.dot(t, x, preferred_element_type=F32))


def rounded(x):
    return (x * (float(K) ** -0.5)).astype(BF16)


def terms(a1, b1, a2, b2):
    re = a1 * a2 + b1 * b2
    im = b1 * a2 - a1 * b2
    pw = (a1 * a1 + b1 * b1 + a2 * a2 + b2 * b2) * 0.5
    return re, im, pw


def outer_kernel(n, kl, first, *refs):
    pieces, t_ref, outs = refs[:n], refs[n], refs[n + 1 :]
    for slot in range(len(first)):
        s = transform(t_ref, pieces, kl, slot)
        outs[slot][: 2 * DEPTH, :] = s[:, :LANES]
        outs[slot][2 * DEPTH : 4 * DEPTH, :] = s[:, LANES:]
    me = lax.axis_index("ka")
    t = jnp.concatenate([t_ref[me ^ s] for s in range(n)], axis=1)
    e = jnp.concatenate([p[len(first) * 2 * kl :, :kl] for p in pieces], axis=1)
    e = jnp.concatenate([e, jnp.zeros((LANES - EDGE, K), BF16)], axis=0)
    se = lax.dot_general(t, e, (((1,), (1,)), ((), ())), preferred_element_type=F32)
    se = rounded(se).astype(F32)
    packed = se[:LANES]
    for b in range(1, 2 * DEPTH // LANES):
        packed = packed + pltpu.roll(se[b * LANES : (b + 1) * LANES], EDGE * b, 1)
    packed = packed.astype(BF16)
    for slot in range(len(first)):
        outs[slot][4 * DEPTH :, :] = packed


def outer(pieces, t, n, kl, first):
    return pl.pallas_call(
        functools.partial(outer_kernel, n, kl, first),
        out_shape=[jax.ShapeDtypeStruct((4 * DEPTH + LANES, LANES), BF16)] * len(first),
        compiler_params=params(),
        cost_estimate=pl.CostEstimate(
            flops=2 * 2 * DEPTH * K * 256 * 3, bytes_accessed=4 * 2**20, transcendentals=0
        ),
        name="outer",
    )(*pieces, t)


def inner_kernel(n, kl, rest, *refs):
    pieces, t_ref, out = refs[:n], refs[n], refs[n + 1]
    for slot in range(len(rest)):
        s = transform(t_ref, pieces, kl, slot)
        out[slot, : 2 * DEPTH, :] = s[:, :LANES]
        out[slot, 2 * DEPTH :, :] = s[:, LANES:]


def inner(pieces, t, n, kl, rest):
    return pl.pallas_call(
        functools.partial(inner_kernel, n, kl, rest),
        out_shape=jax.ShapeDtypeStruct((len(rest), 4 * DEPTH, LANES), BF16),
        compiler_params=params(),
        cost_estimate=pl.CostEstimate(flops=4 * 10**9, bytes_accessed=6 * 2**20, transcendentals=0),
        name="inner",
    )(*pieces, t)


STEP = 16


def box_kernel(n, rb, far, *refs):
    half, span, count = n // 2, DEPTH // 2, 4 + (rb > 2)
    above, top, bottom, below = refs[0], refs[1], refs[count - 2], refs[count - 1]
    inside = refs[2]
    outs = refs[count : count + half] if far else refs[count + 1 : count + 1 + half]
    edge = refs[count + half] if far else refs[count]
    total, dec = refs[-2:]
    me = lax.axis_index("ka")
    h = me // half
    dl = DEPTH // n
    base = pl.multiple_of((1 - h if far else h) * span, span)

    def spectrum(r, z):
        ref = {-1: above, 0: top, rb - 1: bottom, rb: below}.get(r)
        where = [pl.ds(z + j * DEPTH, STEP) for j in range(4)]
        rows = [ref[w, :] for w in where] if ref is not None else [inside[r - 1, w, :] for w in where]
        return [x.astype(F32) for x in rows]

    def make_edge():
        lane = lax.broadcasted_iota(jnp.int32, (LANES, LANES), 1)
        packed = top[4 * DEPTH :, :].astype(F32)
        up = pltpu.roll(above[4 * DEPTH :, :].astype(F32), LANES - rb, 1)
        down = pltpu.roll(below[4 * DEPTH :, :].astype(F32), rb, 1)
        packed = jnp.where(lane % 8 == 0, up, jnp.where(lane % 8 == rb + 1, down, packed))
        blocks = DEPTH // LANES
        sines = pltpu.roll(packed, LANES - EDGE * blocks, 1)
        second = [pltpu.roll(x, LANES - 8, 1) for x in (packed, sines)]
        for t, v in enumerate(terms(packed, sines, *second)):
            v = v + pltpu.roll(v, 1, 1) + pltpu.roll(v, LANES - 1, 1)
            for b in range(blocks):
                turned = pltpu.roll(v, LANES - EDGE * b, 1) if b else v
                edge[t, pl.ds(b * LANES + 8, LANES), :] = turned
        for t in range(3):
            for z in (0, DEPTH + 8):
                edge[t, pl.ds(z, 8), :] = jnp.zeros((8, LANES), F32)

    if far:
        make_edge()

    def over_rows(z, at, keep=None):
        before = terms(*spectrum(-1, z))
        here = terms(*spectrum(0, z))
        pair = [x + y for x, y in zip(before, here)]
        for r in range(rb):
            after = terms(*spectrum(r + 1, z))
            for t in range(3):
                v = pair[t] + after[t]
                v = v if keep is None else jnp.where(keep, v, 0.0)
                total[r, t, pl.ds(at, STEP), :] = v
            pair = [x + y for x, y in zip(here, after)]
            here = after

    @pl.loop(0, span // STEP, unroll=4)
    def _(i):
        z = pl.multiple_of(i * STEP, STEP)
        over_rows(pl.multiple_of(base + z, STEP), pl.multiple_of(z + STEP, STEP))

    z = pl.multiple_of(jnp.maximum(base - STEP, 0), STEP)
    over_rows(z, 0, base > 0)
    z = pl.multiple_of(jnp.minimum(base + span, DEPTH - STEP), STEP)
    over_rows(z, span + STEP, base + span < DEPTH)

    lane = lax.broadcasted_iota(jnp.int32, (STEP, LANES), 1)
    not_first, not_last = lane > 0, lane < LANES - 1
    at_edge = lane == jnp.where(h == 0, LANES - 1, 0)

    def deep(x):
        return x[0] + x[1] + x[2]

    @pl.loop(0, span // STEP, unroll=8)
    def _(i):
        z = pl.multiple_of(i * STEP, STEP)
        rim = [deep([edge[t, pl.ds(base + z + j, STEP), :] for j in (7, 8, 9)]) for t in range(3)]
        for r in range(rb):
            box = []
            for t in range(3):
                v = deep([total[r, t, pl.ds(z + STEP + j, STEP), :] for j in (-1, 0, 1)])
                left = jnp.where(not_first, pltpu.roll(v, 1, 1), 0.0)
                right = jnp.where(not_last, pltpu.roll(v, LANES - 1, 1), 0.0)
                e = jnp.where(at_edge, pltpu.roll(rim[t], LANES - 2 - r + h, 1), 0.0)
                box.append(v + left + right + e)
            square = box[0] * box[0] + box[1] * box[1]
            floor = box[2] + 1e-05
            scaled = jnp.maximum(square, 1e-27) * (floor * floor)
            d = 1.0 - square * lax.rsqrt(scaled)
            dec[r, pl.ds(z, STEP), :] = (d * jnp.abs(d) * (d * d)).astype(BF16)

    for i in range(half):
        z = pl.multiple_of(((me ^ i) % half) * dl, dl)
        for r in range(rb):
            outs[i][pl.ds(r * dl, dl), :] = dec[r, pl.ds(z, dl), :]


def boxed(rows, n, rb, edge=None):
    far = edge is None
    return pl.pallas_call(
        functools.partial(box_kernel, n, rb, far),
        out_shape=[jax.ShapeDtypeStruct((rb * (DEPTH // n), LANES), BF16)] * (n // 2)
        + ([jax.ShapeDtypeStruct((3, DEPTH + 16, LANES), F32)] if far else []),
        scratch_shapes=[
            pltpu.VMEM((rb, 3, DEPTH // 2 + 2 * STEP, LANES), F32),
            pltpu.VMEM((rb, DEPTH // 2, LANES), BF16),
        ],
        compiler_params=params(),
        cost_estimate=pl.CostEstimate(flops=10**7, bytes_accessed=6 * 2**20, transcendentals=0),
        name="boxed",
    )(*rows, *([] if far else [edge]))


def join_kernel(n, rows, rb, far, *refs):
    half = n // 2
    pieces = refs[:half]
    out, held, sem = refs[-3:]
    me = lax.axis_index("ka")
    mirrored = lax.axis_index("row") % 2 == 1
    dl = DEPTH // n
    for i in range(half):
        _, row = place(me ^ i, half, rb, mirrored)
        for r in range(rb):
            coded = pieces[i][pl.ds(r * dl, dl), :].astype(F32)
            d = jnp.sqrt(jnp.sqrt(jnp.abs(coded)))
            d = jnp.where(coded < 0.0, -d, d)
            held[pl.ds(row + r, dl, stride=rows), :] = d
    h = me // half
    column = pl.multiple_of((1 - h if far else h) * LANES, LANES)
    copy = pltpu.make_async_copy(held, out.at[:, pl.ds(column, LANES)], sem)
    copy.start()
    copy.wait()


def join(pieces, n, rows, rb, other=None):
    far = other is None
    half, size = n // 2, DEPTH // n * rows
    return pl.pallas_call(
        functools.partial(join_kernel, n, rows, rb, far),
        out_shape=jax.ShapeDtypeStruct((size, 2 * LANES), F32),
        in_specs=[pl.BlockSpec(memory_space=pltpu.VMEM)] * half
        + ([] if far else [pl.BlockSpec(memory_space=pltpu.HBM)]),
        out_specs=pl.BlockSpec(memory_space=pltpu.HBM),
        input_output_aliases={} if far else {half: 0},
        scratch_shapes=[pltpu.VMEM((size, LANES), F32), pltpu.SemaphoreType.DMA],
        compiler_params=params(),
        cost_estimate=pl.CostEstimate(
            flops=10**9 if far else 10**6, bytes_accessed=2 * 2**20, transcendentals=0
        ),
        name="join",
    )(*pieces, *([] if far else [other]))


def body(frames):
    n, groups = lax.axis_size("ka"), lax.axis_size("row")
    _, kl, rows, cols = frames.shape
    half = n // 2
    rb = rows // half
    first, rest = (0, rb - 1), tuple(range(1, rb - 1))
    t = jnp.asarray(table().reshape(2 * DEPTH, n, kl).transpose(1, 0, 2))

    far, near, core = range(half, n), range(2, half), range(1, 2)

    def exchange(pieces, order):
        out = list(pieces)
        for s in order:
            out[s] = lax.ppermute(pieces[s], "ka", [(i, i ^ s) for i in range(n)])
        return out

    x = pltpu.with_memory_space_constraint(frames.reshape(2 * kl * rows, cols), pltpu.HBM)
    a = exchange(split(x, n, rows, kl, rb, first, True), [*far, *near, *core])
    b = []
    if rest:
        b = exchange(split(x, n, rows, kl, rb, rest, False, [a[[*far, *near, *core][AFTER]]]), [*far, *near, *core])
    top, bottom = outer(a, t, n, kl, first)

    def where(h, block):
        g, q = block // half, block % half
        q = q if g % 2 == 0 else half - 1 - q
        return (h * half + q) * groups + g

    steps = [(h, block) for h in range(2) for block in range(groups * half - 1)]
    down = [(where(h, block), where(h, block + 1)) for h, block in steps]
    above = lax.ppermute(bottom, ("ka", "row"), down)
    below = lax.ppermute(top, ("ka", "row"), [(j, i) for i, j in down])
    inside = [inner(b, t, n, kl, rest)] if rest else []
    spectra = [above, top, *inside, bottom, below]
    *away, edge = boxed(spectra, n, rb)
    pieces = [*boxed(spectra, n, rb, edge), *away]
    pieces = exchange(pieces, [*far, *near, *core])
    out = join(pieces[:half], n, rows, rb, join(pieces[half:], n, rows, rb))
    return out.reshape(DEPTH // n, rows, cols)


def solution(mesh):
    in_specs = (P(None, "ka", "row", None),)
    out_specs = P("ka", "row", None)
    return jax.shard_map(body, mesh=mesh, in_specs=in_specs, out_specs=out_specs, check_vma=False)
```

```python
import functools
import math

import jax
import jax.numpy as jnp
import numpy as np
from jax import lax
from jax.experimental import pallas as pl
from jax.experimental.pallas import tpu as pltpu
from jax.sharding import PartitionSpec as P

K = 1024
DEPTH = 512
LANES = 128
AFTER = 2
STEP = 16
EDGE = 16
F32 = jnp.float32
BF16 = jnp.bfloat16


def table():
    phase = (np.arange(K)[None, :] * np.arange(DEPTH)[:, None]) % K
    angle = phase.astype(np.float32) * np.float32(2.0 * math.pi / K)
    both = np.concatenate([np.cos(angle), np.sin(angle)], axis=0)
    return both.astype(jnp.bfloat16)


def place(dest, half, rb, mirrored):
    h = dest // half
    q = dest % half
    q = jnp.where(mirrored, half - 1 - q, q)
    return h, q * rb


def params(mib=48):
    return pltpu.CompilerParams(vmem_limit_bytes=mib * 1024 * 1024)


def split_kernel(n, rows, kl, rb, group, edge, x_ref, *refs):
    half = n // 2
    outs, held, x32, sem = refs[-n - 3 : -3], refs[-3], refs[-2], refs[-1]
    me = lax.axis_index("ka")
    mirrored = lax.axis_index("row") % 2 == 1
    size = kl * rows
    copies = [
        pltpu.make_async_copy(x_ref.at[pl.ds(p * size, size)], held.at[p], sem.at[p])
        for p in range(2)
    ]
    for c in copies:
        c.start()
    lane = lax.broadcasted_iota(jnp.int32, (kl, LANES), 1)
    edges = [jnp.zeros((kl, LANES), F32) for _ in range(n * EDGE // LANES)]
    for p in range(2):
        copies[p].wait()
        for h in range(2):
            x32[p, h] = held[p, :, h * LANES : (h + 1) * LANES].astype(F32)
        for s in range(n):
            h, row = place(me ^ s, half, rb, mirrored)
            for j in range(rb) if edge else group:
                y = x32[p, h, pl.ds(row + j, kl, stride=rows), :]
                if j in group:
                    slot = group.index(j)
                    outs[s][pl.ds((slot * 2 + p) * kl, kl), :] = y.astype(BF16)
                if edge:
                    m, at = divmod(s * EDGE + p * 8 + 1 + j, LANES)
                    y = pltpu.roll(y, (at + 1 - h) % LANES, 1)
                    edges[m] = jnp.where(lane == at, y, edges[m])
    for m, e in enumerate(edges if edge else []):
        if kl < LANES:
            e = jnp.concatenate([e, jnp.zeros((LANES - kl, LANES), F32)], axis=0)
        e = e.T.astype(BF16)
        for i in range(LANES // EDGE):
            s = (m * LANES // EDGE + i) ^ half
            outs[s][pl.ds(len(group) * 2 * kl, EDGE), :] = e[i * EDGE : (i + 1) * EDGE]


def split(x, n, rows, kl, rb, group, edge, after=()):
    size = len(group) * 2 * kl + (EDGE if edge else 0)
    return pl.pallas_call(
        functools.partial(split_kernel, n, rows, kl, rb, group, edge),
        out_shape=[jax.ShapeDtypeStruct((size, LANES), BF16)] * n,
        in_specs=[pl.BlockSpec(memory_space=pltpu.HBM)]
        + [pl.BlockSpec(memory_space=pl.ANY)] * len(after),
        scratch_shapes=[
            pltpu.VMEM((2, kl * rows, 2 * LANES), BF16),
            pltpu.VMEM((2, 2, kl * rows, LANES), F32),
            pltpu.SemaphoreType.DMA((2,)),
        ],
        compiler_params=params(),
        cost_estimate=pl.CostEstimate(flops=10**6, bytes_accessed=4 * 2**20, transcendentals=0),
        name="split",
    )(x, *after)


def transform(t_ref, pieces, kl, slot, base=None):
    n = len(pieces)
    me = lax.axis_index("ka")
    if base is None:
        blocks = [t_ref[me ^ s] for s in range(n)]
    else:
        span = DEPTH // 2
        other = pl.multiple_of(jnp.where(base == 0, span, span - STEP), STEP)
        parts = [(z + at, size) for z in (0, DEPTH) for at, size in ((base, span), (other, STEP))]
        blocks = [
            jnp.concatenate([t_ref[me ^ s, pl.ds(z, size), :] for z, size in parts], axis=0)
            for s in range(n)
        ]
    t = jnp.concatenate(blocks, axis=1)
    x = jnp.concatenate(
        [
            jnp.concatenate([p[pl.ds((slot * 2 + q) * kl, kl), :] for p in pieces], axis=0)
            for q in range(2)
        ],
        axis=1,
    )
    return rounded(jnp.dot(t, x, preferred_element_type=F32))


def rounded(x):
    return (x * (float(K) ** -0.5)).astype(BF16)


def terms(a1, b1, a2, b2):
    re = a1 * a2 + b1 * b2
    im = b1 * a2 - a1 * b2
    pw = (a1 * a1 + b1 * b1 + a2 * a2 + b2 * b2) * 0.5
    return re, im, pw


def outer_kernel(n, kl, first, *refs):
    pieces, t_ref, outs = refs[:n], refs[n], refs[n + 1 :]
    for slot in range(len(first)):
        s = transform(t_ref, pieces, kl, slot)
        outs[slot][: 2 * DEPTH, :] = s[:, :LANES]
        outs[slot][2 * DEPTH : 4 * DEPTH, :] = s[:, LANES:]
    me = lax.axis_index("ka")
    t = jnp.concatenate([t_ref[me ^ s] for s in range(n)], axis=1)
    e = jnp.concatenate([p[len(first) * 2 * kl :, :kl] for p in pieces], axis=1)
    e = jnp.concatenate([e, jnp.zeros((LANES - EDGE, K), BF16)], axis=0)
    se = lax.dot_general(t, e, (((1,), (1,)), ((), ())), preferred_element_type=F32)
    se = rounded(se).astype(F32)
    packed = se[:LANES]
    for b in range(1, 2 * DEPTH // LANES):
        packed = packed + pltpu.roll(se[b * LANES : (b + 1) * LANES], EDGE * b, 1)
    packed = packed.astype(BF16)
    for slot in range(len(first)):
        outs[slot][4 * DEPTH :, :] = packed


def outer(pieces, t, n, kl, first):
    return pl.pallas_call(
        functools.partial(outer_kernel, n, kl, first),
        out_shape=[jax.ShapeDtypeStruct((4 * DEPTH + LANES, LANES), BF16)] * len(first),
        compiler_params=params(),
        cost_estimate=pl.CostEstimate(
            flops=2 * 2 * DEPTH * K * 256 * 3, bytes_accessed=4 * 2**20, transcendentals=0
        ),
        name="outer",
    )(*pieces, t)


def half_rows(t_ref, pieces, kl, rest, base, out):
    for slot in range(len(rest)):
        s = transform(t_ref, pieces, kl, slot, base)
        out[slot, : DEPTH + 2 * STEP, :] = s[:, :LANES]
        out[slot, DEPTH + 2 * STEP :, :] = s[:, LANES:]


def inner_kernel(n, kl, rest, far, *refs):
    pieces, t_ref, out = refs[:n], refs[n], refs[-1]
    h = lax.axis_index("ka") // (n // 2)
    base = pl.multiple_of((1 - h if far else h) * (DEPTH // 2), DEPTH // 2)
    half_rows(t_ref, pieces, kl, rest, base, out)


def inner(pieces, t, n, kl, rest, after=()):
    return pl.pallas_call(
        functools.partial(inner_kernel, n, kl, rest, not after),
        out_shape=jax.ShapeDtypeStruct((len(rest), 2 * (DEPTH + 2 * STEP), LANES), BF16),
        in_specs=[pl.BlockSpec(memory_space=pltpu.VMEM)] * (n + 1)
        + [pl.BlockSpec(memory_space=pl.ANY)] * len(after),
        compiler_params=params(),
        cost_estimate=pl.CostEstimate(flops=10**7 if after else 4 * 10**9, bytes_accessed=6 * 2**20, transcendentals=0),
        name="inner",
    )(*pieces, t, *after)


def box_kernel(n, kl, rb, far, *refs):
    half, span = n // 2, DEPTH // 2
    above, top, bottom, below = refs[:4]
    own = 0 if far or rb == 2 else 1
    total, dec, inside = refs[-3:]
    if far:
        inside = refs[4] if rb > 2 else None
        outs, edge = refs[-half - 4 : -4], refs[-4]
    else:
        edge, sources = refs[4], refs[5 : 5 + own]
        outs = refs[5 + own : 5 + own + half]
    me = lax.axis_index("ka")
    h = me // half
    dl = DEPTH // n
    base = pl.multiple_of((1 - h if far else h) * span, span)

    if own:
        inside = sources[0]

    def spectrum(r, z, near):
        ref = {-1: above, 0: top, rb - 1: bottom, rb: below}.get(r)
        if ref is not None:
            rows = [ref[pl.ds(z + j * DEPTH, STEP), :] for j in range(4)]
        else:
            rows = [inside[r - 1, pl.ds(near + j * (span + STEP), STEP), :] for j in range(4)]
        return [x.astype(F32) for x in rows]

    def make_edge():
        lane = lax.broadcasted_iota(jnp.int32, (LANES, LANES), 1)
        packed = top[4 * DEPTH :, :].astype(F32)
        up = pltpu.roll(above[4 * DEPTH :, :].astype(F32), LANES - rb, 1)
        down = pltpu.roll(below[4 * DEPTH :, :].astype(F32), rb, 1)
        packed = jnp.where(lane % 8 == 0, up, jnp.where(lane % 8 == rb + 1, down, packed))
        blocks = DEPTH // LANES
        sines = pltpu.roll(packed, LANES - EDGE * blocks, 1)
        second = [pltpu.roll(x, LANES - 8, 1) for x in (packed, sines)]
        for t, v in enumerate(terms(packed, sines, *second)):
            v = v + pltpu.roll(v, 1, 1) + pltpu.roll(v, LANES - 1, 1)
            for b in range(blocks):
                turned = pltpu.roll(v, LANES - EDGE * b, 1) if b else v
                edge[t, pl.ds(b * LANES + 8, LANES), :] = turned
        for t in range(3):
            for z in (0, DEPTH + 8):
                edge[t, pl.ds(z, 8), :] = jnp.zeros((8, LANES), F32)

    if far:
        make_edge()

    def over_rows(z, at, near, keep=None):
        before = terms(*spectrum(-1, z, near))
        here = terms(*spectrum(0, z, near))
        pair = [x + y for x, y in zip(before, here)]
        for r in range(rb):
            after = terms(*spectrum(r + 1, z, near))
            for t in range(3):
                v = pair[t] + after[t]
                v = v if keep is None else jnp.where(keep, v, 0.0)
                total[r, t, pl.ds(at, STEP), :] = v
            pair = [x + y for x, y in zip(here, after)]
            here = after

    @pl.loop(0, span // STEP, unroll=4)
    def _(i):
        z = pl.multiple_of(i * STEP, STEP)
        over_rows(pl.multiple_of(base + z, STEP), pl.multiple_of(z + STEP, STEP), z)

    z = pl.multiple_of(jnp.maximum(base - STEP, 0), STEP)
    over_rows(z, 0, span, base > 0)
    z = pl.multiple_of(jnp.minimum(base + span, DEPTH - STEP), STEP)
    over_rows(z, span + STEP, span, base + span < DEPTH)

    lane = lax.broadcasted_iota(jnp.int32, (STEP, LANES), 1)
    not_first, not_last = lane > 0, lane < LANES - 1
    at_edge = lane == jnp.where(h == 0, LANES - 1, 0)

    def deep(x):
        return x[0] + x[1] + x[2]

    @pl.loop(0, span // STEP, unroll=8)
    def _(i):
        z = pl.multiple_of(i * STEP, STEP)
        rim = [deep([edge[t, pl.ds(base + z + j, STEP), :] for j in (7, 8, 9)]) for t in range(3)]
        for r in range(rb):
            box = []
            for t in range(3):
                v = deep([total[r, t, pl.ds(z + STEP + j, STEP), :] for j in (-1, 0, 1)])
                left = jnp.where(not_first, pltpu.roll(v, 1, 1), 0.0)
                right = jnp.where(not_last, pltpu.roll(v, LANES - 1, 1), 0.0)
                e = jnp.where(at_edge, pltpu.roll(rim[t], LANES - 2 - r + h, 1), 0.0)
                box.append(v + left + right + e)
            square = box[0] * box[0] + box[1] * box[1]
            floor = box[2] + 1e-05
            scaled = jnp.maximum(square, 1e-27) * (floor * floor)
            d = 1.0 - square * lax.rsqrt(scaled)
            dec[r, pl.ds(z, STEP), :] = (d * jnp.abs(d) * (d * d)).astype(BF16)

    for i in range(half):
        z = pl.multiple_of(((me ^ i) % half) * dl, dl)
        for r in range(rb):
            outs[i][pl.ds(r * dl, dl), :] = dec[r, pl.ds(z, dl), :]


def boxed(rows, n, kl, rb, far):
    return pl.pallas_call(
        functools.partial(box_kernel, n, kl, rb, far),
        out_shape=[jax.ShapeDtypeStruct((rb * (DEPTH // n), LANES), BF16)] * (n // 2)
        + ([jax.ShapeDtypeStruct((3, DEPTH + 16, LANES), F32)] if far else []),
        scratch_shapes=[
            pltpu.VMEM((rb, 3, DEPTH // 2 + 2 * STEP, LANES), F32),
            pltpu.VMEM((rb, DEPTH // 2, LANES), BF16),
            pltpu.VMEM((max(rb - 2, 1), 16 if far else 2 * (DEPTH + 2 * STEP), LANES), BF16),
        ],
        compiler_params=params(),
        cost_estimate=pl.CostEstimate(flops=10**7, bytes_accessed=6 * 2**20, transcendentals=0),
        name="boxed",
    )(*rows)


def join_kernel(n, rows, rb, far, *refs):
    half = n // 2
    pieces = refs[:half]
    out, held, sem = refs[-3:]
    me = lax.axis_index("ka")
    mirrored = lax.axis_index("row") % 2 == 1
    dl = DEPTH // n
    for i in range(half):
        _, row = place(me ^ i, half, rb, mirrored)
        for r in range(rb):
            coded = pieces[i][pl.ds(r * dl, dl), :].astype(F32)
            d = jnp.sqrt(jnp.sqrt(jnp.abs(coded)))
            d = jnp.where(coded < 0.0, -d, d)
            held[pl.ds(row + r, dl, stride=rows), :] = d
    h = me // half
    column = pl.multiple_of((1 - h if far else h) * LANES, LANES)
    copy = pltpu.make_async_copy(held, out.at[:, pl.ds(column, LANES)], sem)
    copy.start()
    copy.wait()


def join(pieces, n, rows, rb, other=None):
    far = other is None
    half, size = n // 2, DEPTH // n * rows
    return pl.pallas_call(
        functools.partial(join_kernel, n, rows, rb, far),
        out_shape=jax.ShapeDtypeStruct((size, 2 * LANES), F32),
        in_specs=[pl.BlockSpec(memory_space=pltpu.VMEM)] * half
        + ([] if far else [pl.BlockSpec(memory_space=pltpu.HBM)]),
        out_specs=pl.BlockSpec(memory_space=pltpu.HBM),
        input_output_aliases={} if far else {half: 0},
        scratch_shapes=[pltpu.VMEM((size, LANES), F32), pltpu.SemaphoreType.DMA],
        compiler_params=params(),
        cost_estimate=pl.CostEstimate(
            flops=10**9 if far else 10**6, bytes_accessed=2 * 2**20, transcendentals=0
        ),
        name="join",
    )(*pieces, *([] if far else [other]))


def body(frames):
    n, groups = lax.axis_size("ka"), lax.axis_size("row")
    _, kl, rows, cols = frames.shape
    half = n // 2
    rb = rows // half
    first, rest = (0, rb - 1), tuple(range(1, rb - 1))
    t = jnp.asarray(table().reshape(2 * DEPTH, n, kl).transpose(1, 0, 2))

    far, near, core = range(half, n), range(2, half), range(1, 2)

    def exchange(pieces, order):
        out = list(pieces)
        for s in order:
            out[s] = lax.ppermute(pieces[s], "ka", [(i, i ^ s) for i in range(n)])
        return out

    x = pltpu.with_memory_space_constraint(frames.reshape(2 * kl * rows, cols), pltpu.HBM)
    a = exchange(split(x, n, rows, kl, rb, first, True), [*far, *near, *core])
    b = []
    if rest:
        b = exchange(split(x, n, rows, kl, rb, rest, False, [a[[*far, *near, *core][AFTER]]]), [*far, *near, *core])
    top, bottom = outer(a, t, n, kl, first)

    def where(h, block):
        g, q = block // half, block % half
        q = q if g % 2 == 0 else half - 1 - q
        return (h * half + q) * groups + g

    steps = [(h, block) for h in range(2) for block in range(groups * half - 1)]
    down = [(where(h, block), where(h, block + 1)) for h, block in steps]
    above = lax.ppermute(bottom, ("ka", "row"), down)
    below = lax.ppermute(top, ("ka", "row"), [(j, i) for i, j in down])
    inside = [inner(b, t, n, kl, rest)] if rest else []
    outside = [above, top, bottom, below]
    *away, edge = boxed([*outside, *inside], n, kl, rb, True)
    here = boxed([*outside, edge, *([inner(b, t, n, kl, rest, [edge])] if rest else [])], n, kl, rb, False)
    pieces = [*here, *away]
    pieces = exchange(pieces, [*far, *near, *core])
    out = join(pieces[:half], n, rows, rb, join(pieces[half:], n, rows, rb))
    return out.reshape(DEPTH // n, rows, cols)


def solution(mesh):
    in_specs = (P(None, "ka", "row", None),)
    out_specs = P("ka", "row", None)
    return jax.shard_map(body, mesh=mesh, in_specs=in_specs, out_specs=out_specs, check_vma=False)
```

```python
import functools
import math

import jax
import jax.numpy as jnp
import numpy as np
from jax import lax
from jax.experimental import pallas as pl
from jax.experimental.pallas import tpu as pltpu
from jax.sharding import PartitionSpec as P

K = 1024
DEPTH = 512
LANES = 128
AFTER = 2
STEP = 16
EDGE = 16
F32 = jnp.float32
BF16 = jnp.bfloat16


def table():
    phase = (np.arange(K)[None, :] * np.arange(DEPTH)[:, None]) % K
    angle = phase.astype(np.float32) * np.float32(2.0 * math.pi / K)
    both = np.concatenate([np.cos(angle), np.sin(angle)], axis=0)
    return both.astype(jnp.bfloat16)


def place(dest, half, rb, mirrored):
    h = dest // half
    q = dest % half
    q = jnp.where(mirrored, half - 1 - q, q)
    return h, q * rb


def params(mib=48):
    return pltpu.CompilerParams(vmem_limit_bytes=mib * 1024 * 1024)


def split_kernel(n, rows, kl, rb, group, edge, x_ref, *refs):
    half = n // 2
    outs, held, x32, sem = refs[-n - 3 : -3], refs[-3], refs[-2], refs[-1]
    me = lax.axis_index("ka")
    mirrored = lax.axis_index("row") % 2 == 1
    size = kl * rows
    copies = [
        pltpu.make_async_copy(x_ref.at[pl.ds(p * size, size)], held.at[p], sem.at[p])
        for p in range(2)
    ]
    for c in copies:
        c.start()
    lane = lax.broadcasted_iota(jnp.int32, (kl, LANES), 1)
    edges = [jnp.zeros((kl, LANES), F32) for _ in range(n * EDGE // LANES)]
    for p in range(2):
        copies[p].wait()
        for h in range(2):
            x32[p, h] = held[p, :, h * LANES : (h + 1) * LANES].astype(F32)
        for s in range(n):
            h, row = place(me ^ s, half, rb, mirrored)
            for j in range(rb) if edge else group:
                y = x32[p, h, pl.ds(row + j, kl, stride=rows), :]
                if j in group:
                    slot = group.index(j)
                    outs[s][pl.ds((slot * 2 + p) * kl, kl), :] = y.astype(BF16)
                if edge:
                    m, at = divmod(s * EDGE + p * 8 + 1 + j, LANES)
                    y = pltpu.roll(y, (at + 1 - h) % LANES, 1)
                    edges[m] = jnp.where(lane == at, y, edges[m])
    for m, e in enumerate(edges if edge else []):
        if kl < LANES:
            e = jnp.concatenate([e, jnp.zeros((LANES - kl, LANES), F32)], axis=0)
        e = e.T.astype(BF16)
        for i in range(LANES // EDGE):
            s = (m * LANES // EDGE + i) ^ half
            outs[s][pl.ds(len(group) * 2 * kl, EDGE), :] = e[i * EDGE : (i + 1) * EDGE]


def split(x, n, rows, kl, rb, group, edge, after=()):
    size = len(group) * 2 * kl + (EDGE if edge else 0)
    return pl.pallas_call(
        functools.partial(split_kernel, n, rows, kl, rb, group, edge),
        out_shape=[jax.ShapeDtypeStruct((size, LANES), BF16)] * n,
        in_specs=[pl.BlockSpec(memory_space=pltpu.HBM)]
        + [pl.BlockSpec(memory_space=pl.ANY)] * len(after),
        scratch_shapes=[
            pltpu.VMEM((2, kl * rows, 2 * LANES), BF16),
            pltpu.VMEM((2, 2, kl * rows, LANES), F32),
            pltpu.SemaphoreType.DMA((2,)),
        ],
        compiler_params=params(),
        cost_estimate=pl.CostEstimate(flops=10**6, bytes_accessed=4 * 2**20, transcendentals=0),
        name="split",
    )(x, *after)


def transform(t_ref, pieces, kl, slot, base=None):
    n = len(pieces)
    me = lax.axis_index("ka")
    if base is None:
        blocks = [t_ref[me ^ s] for s in range(n)]
    else:
        span = DEPTH // 2
        other = pl.multiple_of(jnp.where(base == 0, span, span - STEP), STEP)
        parts = [(z + at, size) for z in (0, DEPTH) for at, size in ((base, span), (other, STEP))]
        blocks = [
            jnp.concatenate([t_ref[me ^ s, pl.ds(z, size), :] for z, size in parts], axis=0)
            for s in range(n)
        ]
    t = jnp.concatenate(blocks, axis=1)
    x = jnp.concatenate(
        [
            jnp.concatenate([p[pl.ds((slot * 2 + q) * kl, kl), :] for p in pieces], axis=0)
            for q in range(2)
        ],
        axis=1,
    )
    return rounded(jnp.dot(t, x, preferred_element_type=F32))


def rounded(x):
    return (x * (float(K) ** -0.5)).astype(BF16)


def terms(a1, b1, a2, b2):
    re = a1 * a2 + b1 * b2
    im = b1 * a2 - a1 * b2
    pw = (a1 * a1 + b1 * b1 + a2 * a2 + b2 * b2) * 0.5
    return re, im, pw


def outer_kernel(n, kl, first, *refs):
    pieces, t_ref, outs = refs[:n], refs[n], refs[n + 1 :]
    for slot in range(len(first)):
        s = transform(t_ref, pieces, kl, slot)
        outs[slot][: 2 * DEPTH, :] = s[:, :LANES]
        outs[slot][2 * DEPTH : 4 * DEPTH, :] = s[:, LANES:]
    me = lax.axis_index("ka")
    t = jnp.concatenate([t_ref[me ^ s] for s in range(n)], axis=1)
    e = jnp.concatenate([p[len(first) * 2 * kl :, :kl] for p in pieces], axis=1)
    e = jnp.concatenate([e, jnp.zeros((LANES - EDGE, K), BF16)], axis=0)
    se = lax.dot_general(t, e, (((1,), (1,)), ((), ())), preferred_element_type=F32)
    se = rounded(se).astype(F32)
    packed = se[:LANES]
    for b in range(1, 2 * DEPTH // LANES):
        packed = packed + pltpu.roll(se[b * LANES : (b + 1) * LANES], EDGE * b, 1)
    packed = packed.astype(BF16)
    for slot in range(len(first)):
        outs[slot][4 * DEPTH :, :] = packed


def outer(pieces, t, n, kl, first):
    return pl.pallas_call(
        functools.partial(outer_kernel, n, kl, first),
        out_shape=[jax.ShapeDtypeStruct((4 * DEPTH + LANES, LANES), BF16)] * len(first),
        compiler_params=params(),
        cost_estimate=pl.CostEstimate(
            flops=2 * 2 * DEPTH * K * 256 * 3, bytes_accessed=4 * 2**20, transcendentals=0
        ),
        name="outer",
    )(*pieces, t)


def half_rows(t_ref, pieces, kl, rest, base, out):
    for slot in range(len(rest)):
        s = transform(t_ref, pieces, kl, slot, base)
        out[slot, : DEPTH + 2 * STEP, :] = s[:, :LANES]
        out[slot, DEPTH + 2 * STEP :, :] = s[:, LANES:]


def inner_kernel(n, kl, rest, far, *refs):
    pieces, t_ref, out = refs[:n], refs[n], refs[-1]
    h = lax.axis_index("ka") // (n // 2)
    base = pl.multiple_of((1 - h if far else h) * (DEPTH // 2), DEPTH // 2)
    half_rows(t_ref, pieces, kl, rest, base, out)


def inner(pieces, t, n, kl, rest, after=()):
    return pl.pallas_call(
        functools.partial(inner_kernel, n, kl, rest, not after),
        out_shape=jax.ShapeDtypeStruct((len(rest), 2 * (DEPTH + 2 * STEP), LANES), BF16),
        in_specs=[pl.BlockSpec(memory_space=pltpu.VMEM)] * (n + 1)
        + [pl.BlockSpec(memory_space=pl.ANY)] * len(after),
        compiler_params=params(),
        cost_estimate=pl.CostEstimate(flops=10**7 if after else 4 * 10**9, bytes_accessed=6 * 2**20, transcendentals=0),
        name="inner",
    )(*pieces, t, *after)


def box_kernel(n, kl, rb, far, *refs):
    half, span = n // 2, DEPTH // 2
    above, top, bottom, below = refs[:4]
    own = 0 if far or rb == 2 else 1
    total, dec, inside = refs[-3:]
    if far:
        inside = refs[4] if rb > 2 else None
        outs, edge = refs[-half - 4 : -4], refs[-4]
    else:
        edge, sources = refs[4], refs[5 : 5 + own]
        outs = refs[5 + own : 5 + own + half]
    me = lax.axis_index("ka")
    h = me // half
    dl = DEPTH // n
    base = pl.multiple_of((1 - h if far else h) * span, span)

    if own:
        inside = sources[0]

    def spectrum(r, z, near):
        ref = {-1: above, 0: top, rb - 1: bottom, rb: below}.get(r)
        if ref is not None:
            rows = [ref[pl.ds(z + j * DEPTH, STEP), :] for j in range(4)]
        else:
            rows = [inside[r - 1, pl.ds(near + j * (span + STEP), STEP), :] for j in range(4)]
        return [x.astype(F32) for x in rows]

    def make_edge():
        lane = lax.broadcasted_iota(jnp.int32, (LANES, LANES), 1)
        packed = top[4 * DEPTH :, :].astype(F32)
        up = pltpu.roll(above[4 * DEPTH :, :].astype(F32), LANES - rb, 1)
        down = pltpu.roll(below[4 * DEPTH :, :].astype(F32), rb, 1)
        packed = jnp.where(lane % 8 == 0, up, jnp.where(lane % 8 == rb + 1, down, packed))
        blocks = DEPTH // LANES
        sines = pltpu.roll(packed, LANES - EDGE * blocks, 1)
        second = [pltpu.roll(x, LANES - 8, 1) for x in (packed, sines)]
        for t, v in enumerate(terms(packed, sines, *second)):
            v = v + pltpu.roll(v, 1, 1) + pltpu.roll(v, LANES - 1, 1)
            for b in range(blocks):
                turned = pltpu.roll(v, LANES - EDGE * b, 1) if b else v
                edge[t, pl.ds(b * LANES + 8, LANES), :] = turned
        for t in range(3):
            for z in (0, DEPTH + 8):
                edge[t, pl.ds(z, 8), :] = jnp.zeros((8, LANES), F32)

    if far:
        make_edge()

    def over_rows(z, at, near, keep=None):
        before = terms(*spectrum(-1, z, near))
        here = terms(*spectrum(0, z, near))
        pair = [x + y for x, y in zip(before, here)]
        for r in range(rb):
            after = terms(*spectrum(r + 1, z, near))
            for t in range(3):
                v = pair[t] + after[t]
                v = v if keep is None else jnp.where(keep, v, 0.0)
                total[r, t, pl.ds(at, STEP), :] = v
            pair = [x + y for x, y in zip(here, after)]
            here = after

    @pl.loop(0, span // STEP, unroll=8)
    def _(i):
        z = pl.multiple_of(i * STEP, STEP)
        over_rows(pl.multiple_of(base + z, STEP), pl.multiple_of(z + STEP, STEP), z)

    z = pl.multiple_of(jnp.maximum(base - STEP, 0), STEP)
    over_rows(z, 0, span, base > 0)
    z = pl.multiple_of(jnp.minimum(base + span, DEPTH - STEP), STEP)
    over_rows(z, span + STEP, span, base + span < DEPTH)

    lane = lax.broadcasted_iota(jnp.int32, (STEP, LANES), 1)
    not_first, not_last = lane > 0, lane < LANES - 1
    at_edge = lane == jnp.where(h == 0, LANES - 1, 0)

    def deep(x):
        return x[0] + x[1] + x[2]

    @pl.loop(0, span // STEP, unroll=16)
    def _(i):
        z = pl.multiple_of(i * STEP, STEP)
        rim = [deep([edge[t, pl.ds(base + z + j, STEP), :] for j in (7, 8, 9)]) for t in range(3)]
        for r in range(rb):
            box = []
            for t in range(3):
                v = deep([total[r, t, pl.ds(z + STEP + j, STEP), :] for j in (-1, 0, 1)])
                left = jnp.where(not_first, pltpu.roll(v, 1, 1), 0.0)
                right = jnp.where(not_last, pltpu.roll(v, LANES - 1, 1), 0.0)
                e = jnp.where(at_edge, pltpu.roll(rim[t], LANES - 2 - r + h, 1), 0.0)
                box.append(v + left + right + e)
            square = box[0] * box[0] + box[1] * box[1]
            floor = box[2] + 1e-05
            scaled = jnp.maximum(square, 1e-27) * (floor * floor)
            d = 1.0 - square * lax.rsqrt(scaled)
            dec[r, pl.ds(z, STEP), :] = (d * jnp.abs(d) * (d * d)).astype(BF16)

    for i in range(half):
        z = pl.multiple_of(((me ^ i) % half) * dl, dl)
        for r in range(rb):
            outs[i][pl.ds(r * dl, dl), :] = dec[r, pl.ds(z, dl), :]


def boxed(rows, n, kl, rb, far):
    return pl.pallas_call(
        functools.partial(box_kernel, n, kl, rb, far),
        out_shape=[jax.ShapeDtypeStruct((rb * (DEPTH // n), LANES), BF16)] * (n // 2)
        + ([jax.ShapeDtypeStruct((3, DEPTH + 16, LANES), F32)] if far else []),
        scratch_shapes=[
            pltpu.VMEM((rb, 3, DEPTH // 2 + 2 * STEP, LANES), F32),
            pltpu.VMEM((rb, DEPTH // 2, LANES), BF16),
            pltpu.VMEM((max(rb - 2, 1), 16 if far else 2 * (DEPTH + 2 * STEP), LANES), BF16),
        ],
        compiler_params=params(),
        cost_estimate=pl.CostEstimate(flops=10**7, bytes_accessed=6 * 2**20, transcendentals=0),
        name="boxed",
    )(*rows)


def join_kernel(n, rows, rb, far, *refs):
    half = n // 2
    pieces = refs[:half]
    out, held, sem = refs[-3:]
    me = lax.axis_index("ka")
    mirrored = lax.axis_index("row") % 2 == 1
    dl = DEPTH // n
    for i in range(half):
        _, row = place(me ^ i, half, rb, mirrored)
        for r in range(rb):
            coded = pieces[i][pl.ds(r * dl, dl), :].astype(F32)
            d = jnp.sqrt(jnp.sqrt(jnp.abs(coded)))
            d = jnp.where(coded < 0.0, -d, d)
            held[pl.ds(row + r, dl, stride=rows), :] = d
    h = me // half
    column = pl.multiple_of((1 - h if far else h) * LANES, LANES)
    copy = pltpu.make_async_copy(held, out.at[:, pl.ds(column, LANES)], sem)
    copy.start()
    copy.wait()


def join(pieces, n, rows, rb, other=None):
    far = other is None
    half, size = n // 2, DEPTH // n * rows
    return pl.pallas_call(
        functools.partial(join_kernel, n, rows, rb, far),
        out_shape=jax.ShapeDtypeStruct((size, 2 * LANES), F32),
        in_specs=[pl.BlockSpec(memory_space=pltpu.VMEM)] * half
        + ([] if far else [pl.BlockSpec(memory_space=pltpu.HBM)]),
        out_specs=pl.BlockSpec(memory_space=pltpu.HBM),
        input_output_aliases={} if far else {half: 0},
        scratch_shapes=[pltpu.VMEM((size, LANES), F32), pltpu.SemaphoreType.DMA],
        compiler_params=params(),
        cost_estimate=pl.CostEstimate(
            flops=10**9 if far else 10**6, bytes_accessed=2 * 2**20, transcendentals=0
        ),
        name="join",
    )(*pieces, *([] if far else [other]))


def body(frames):
    n, groups = lax.axis_size("ka"), lax.axis_size("row")
    _, kl, rows, cols = frames.shape
    half = n // 2
    rb = rows // half
    first, rest = (0, rb - 1), tuple(range(1, rb - 1))
    t = jnp.asarray(table().reshape(2 * DEPTH, n, kl).transpose(1, 0, 2))

    far, near, core = range(half, n), range(2, half), range(1, 2)

    def exchange(pieces, order):
        out = list(pieces)
        for s in order:
            out[s] = lax.ppermute(pieces[s], "ka", [(i, i ^ s) for i in range(n)])
        return out

    x = pltpu.with_memory_space_constraint(frames.reshape(2 * kl * rows, cols), pltpu.HBM)
    a = exchange(split(x, n, rows, kl, rb, first, True), [*far, *near, *core])
    b = []
    if rest:
        b = exchange(split(x, n, rows, kl, rb, rest, False, [a[[*far, *near, *core][AFTER]]]), [*far, *near, *core])
    top, bottom = outer(a, t, n, kl, first)

    def where(h, block):
        g, q = block // half, block % half
        q = q if g % 2 == 0 else half - 1 - q
        return (h * half + q) * groups + g

    steps = [(h, block) for h in range(2) for block in range(groups * half - 1)]
    down = [(where(h, block), where(h, block + 1)) for h, block in steps]
    above = lax.ppermute(bottom, ("ka", "row"), down)
    below = lax.ppermute(top, ("ka", "row"), [(j, i) for i, j in down])
    inside = [inner(b, t, n, kl, rest)] if rest else []
    outside = [above, top, bottom, below]
    *away, edge = boxed([*outside, *inside], n, kl, rb, True)
    here = boxed([*outside, edge, *([inner(b, t, n, kl, rest, [edge])] if rest else [])], n, kl, rb, False)
    pieces = [*here, *away]
    pieces = exchange(pieces, [*far, *near, *core])
    out = join(pieces[:half], n, rows, rb, join(pieces[half:], n, rows, rb))
    return out.reshape(DEPTH // n, rows, cols)


def solution(mesh):
    in_specs = (P(None, "ka", "row", None),)
    out_specs = P("ka", "row", None)
    return jax.shard_map(body, mesh=mesh, in_specs=in_specs, out_specs=out_specs, check_vma=False)
```
